32 devices in a mesh: dom: 8 (over y, x, core), space: 4 (over z).
Axes of the slice: x: 2, y: 2, z: 4, core: 2. Of those that a mesh axis runs over, the one named last changes fastest.
Arguments:
- ancestor: int32 [32], replicated, may hold values from 0 to 31, as said below
- state: float32 [32, 3, 64, 2048], P('dom', None, 'space'), may hold values from -6 to 6
- jitter: float32 [32, 3, 64, 2048], P('dom', None, 'space'), may hold values from -4 to 4
- depth: float32 [64, 2048], P('space'), may hold values from 0.5 to 2
- coriolis: float32 [64, 2048], P('space'), may hold values from -1 to 1
- drag: float32 [64, 2048], P('space'), may hold values from 0.1 to 1
Outputs:
- forecast: float32 [32, 3, 64, 2048], P('dom', None, 'space')
The draws below stay inside these ranges and needn't reach their ends.
Inputs may be any that keep to these rules, and one draw needn't show every extreme that they name: In-place replacement: every particle either keeps its slot (ancestor[j] = j) or is replaced by a survivor p with ancestor[p] = p and p != j; a survivor is the ancestor of at most two new particles. Among the particles k*4 to k*4 + 3, at most 2 are ancestors of a particle other than themselves, and in every draw some such block has exactly 2.
All inputs are finite; a program needn't handle non-finite values.
Results may differ from the reference program's by a relative error of at most 0.00007.
Values sent between devices are 32-bit elements; how exact they have to be, the bound alone decides.
A program may use at most 128 MiB of HBM per device.

```python
import math
import jax
import jax.numpy as jnp
from jax import lax

PART_DEV = 4
CAP = 2
NX = 2048
STEPS = 4
PART = 32
NY = 64


def draw_ancestor(key, part):
    groups = PART // PART_DEV
    index = jnp.arange(PART, dtype=jnp.int32)
    group_of = index // PART_DEV
    counts = jax.random.randint(jax.random.fold_in(key, 1), (groups,), 0, CAP + 1).astype(jnp.int32)
    counts = counts.at[0].set(CAP)
    scores = jax.random.randint(jax.random.fold_in(key, 2), (PART,), 0, 1 << 20).astype(jnp.int32) * PART + index
    same_group = group_of[:, None] == group_of[None, :]
    rank = jnp.sum((same_group & (scores[None, :] < scores[:, None])).astype(jnp.int32), axis=1)
    donor = rank < counts[group_of]
    donor_int = donor.astype(jnp.int32)
    total = jnp.sum(donor_int)
    kill_score = jax.random.randint(jax.random.fold_in(key, 3), (PART,), 0, 1 << 20).astype(jnp.int32) * PART + index
    kill_score = kill_score + donor_int * (1 << 30)
    kill_pos = jnp.sum((kill_score[None, :] < kill_score[:, None]).astype(jnp.int32), axis=1)
    killed = kill_pos < total
    donor_pos = jnp.cumsum(donor_int) - 1
    match = donor[None, :] & (donor_pos[None, :] == index[:, None])
    donor_of = jnp.sum(jnp.where(match, index[None, :], 0), axis=1).astype(jnp.int32)
    chosen = donor_of[jnp.clip(kill_pos, 0, PART - 1)]
    return jnp.where(killed, chosen, index).astype(jnp.int32)


def block_scale(stream_key, extent, pieces, low, high):
    loudness, own = 1.0, jax.random.fold_in(stream_key, 6)
    for position, parts in pieces:
        steps = jnp.exp(jax.random.uniform(jax.random.fold_in(own, position), (parts,), jnp.float32, low / len(pieces), high / len(pieces)))
        loudness = loudness * jnp.repeat(steps, extent[position] // parts).reshape([-1 if axis == position else 1 for axis in range(len(extent))])
    return loudness


def bell_draw(stream_key, shape, width, limit, pieces=(), kind=jnp.bfloat16):
    values = width * jax.random.normal(stream_key, shape, jnp.float32)
    if pieces:
        values = values * block_scale(stream_key, shape, pieces, -0.22, 0.18)
    return jnp.clip(values, -limit, limit).astype(kind)


def setup_inputs(seed: int = 0) -> dict:
    key_of = jax.random.split(jax.random.key(seed), 7)
    return {
        "ancestor": draw_ancestor(jax.random.fold_in(key_of[6], 71), 0),
        "state": bell_draw(key_of[1], (PART, 3, NY, NX), 1.0, 6.0, ((0, 8), (2, 4)), jnp.float32),
        "jitter": bell_draw(key_of[2], (PART, 3, NY, NX), 0.3, 4.0, ((0, 8), (2, 4)), jnp.float32),
        "depth": jnp.clip(jnp.exp(math.log(2.0) - 1.3862944 * jax.random.uniform(key_of[3], (NY, NX), jnp.float32) ** block_scale(key_of[3], (NY, NX), ((0, 4),), -0.2, 0.2)), 0.5, 2.0),
        "coriolis": jnp.clip(jax.random.uniform(key_of[4], (NY, NX), jnp.float32, -1.0, 1.0) * block_scale(key_of[4], (NY, NX), ((0, 4),), -0.4, 0.0), -1.0, 1.0),
        "drag": jnp.clip(jnp.exp(math.log(1.0) - 2.3025851 * jax.random.uniform(key_of[5], (NY, NX), jnp.float32) ** block_scale(key_of[5], (NY, NX), ((0, 4),), -0.2, 0.2)), 0.1, 1.0),
    }


time_step = 0.3


def diff_zero(values):
    padded = jnp.pad(values, [(0, 0)] * (values.ndim - 1) + [(1, 1)])
    return 0.5 * (padded[..., 2:] - padded[..., :-2])


def diff_edge(values):
    padded = jnp.pad(values, [(0, 0)] * (values.ndim - 1) + [(1, 1)], mode="edge")
    return 0.5 * (padded[..., 2:] - padded[..., :-2])


def advance(fields, depth, coriolis, drag):
    height, across, along = fields[0], fields[1], fields[2]
    for count in range(STEPS):
        flux = depth * along
        height_new = height - time_step * (diff_zero(depth * across) + 0.5 * (jnp.roll(flux, -1, 0) - jnp.roll(flux, 1, 0)))
        across_new = (across + time_step * (coriolis * along - diff_edge(height_new))) / (1.0 + time_step * drag)
        along_new = (along + time_step * (-coriolis * across - 0.5 * (jnp.roll(height_new, -1, 0) - jnp.roll(height_new, 1, 0)))) / (1.0 + time_step * drag)
        height, across, along = height_new, across_new, along_new
    return jnp.stack([height, across, along])


def reference(ancestor, state, jitter, depth, coriolis, drag):
    def member(inputs):
        source, noise = inputs
        fields = lax.dynamic_index_in_dim(state, source, 0, keepdims=False) + noise
        return advance(fields, depth, coriolis, drag)

    return lax.map(member, (ancestor, jitter))
```

```python
import functools

import jax
import jax.numpy as jnp
from jax import lax
from jax.experimental import pallas as pl
from jax.experimental.pallas import tpu as pltpu
from jax.sharding import PartitionSpec as P

STEPS = 4
DT = 0.3
CAP = 2
MESH = pl.DeviceIdType.MESH
UP, DOWN = 0, 1


def column_difference(a, edge):
    width = a.shape[1]
    column = lax.broadcasted_iota(jnp.int32, a.shape, 1)
    beyond = a if edge else jnp.zeros_like(a)
    after = jnp.where(column == width - 1, beyond, pltpu.roll(a, width - 1, 1))
    before = jnp.where(column == 0, beyond, pltpu.roll(a, 1, 1))
    return after - before


def row_difference(a, above, below):
    rows = a.shape[0]
    row = lax.broadcasted_iota(jnp.int32, a.shape, 0)
    after = jnp.where(row == rows - 1, below, pltpu.roll(a, rows - 1, 0))
    before = jnp.where(row == 0, above, pltpu.roll(a, 1, 0))
    return after - before


def advance_kernel(
    count, groups,
    copied, jitter, depth, coriolis, drag, out,
    flux_c, keep_c, turn_c, push_c, rim_send, rim_recv, send, recv, last_send, last_recv, halo,
    send_sem, recv_sem,
):
    members, _, rows, width = out.shape
    each = members // groups
    me = lax.axis_index("space")
    above, below = lax.rem(me + count - 1, count), lax.rem(me + 1, count)
    towards = (above, below)

    barrier = pltpu.get_barrier_semaphore()
    for neighbour in towards:
        pl.semaphore_signal(barrier, inc=1, device_id={"space": neighbour}, device_id_type=MESH)

    def exchange(number, source, target, side):
        return pltpu.make_async_remote_copy(
            src_ref=source, dst_ref=target,
            send_sem=send_sem.at[number, side], recv_sem=recv_sem.at[number, 1 - side],
            device_id={"space": towards[side]}, device_id_type=MESH,
        )

    def rim(side):
        return exchange(0, rim_send.at[side], rim_recv.at[1 - side], side)

    def swap(step, group, side):
        number = 1 + step * groups + group
        if step == STEPS:
            return exchange(number, last_send.at[group, side], last_recv.at[group, 1 - side], side)
        return exchange(number, send.at[step, group, side], recv.at[step, group, 1 - side], side)

    for side, row in ((UP, 0), (DOWN, rows - 1)):
        for k, plane in enumerate((depth, coriolis, drag, drag)):
            rim_send[side, k : k + 1, :] = plane[row : row + 1, :]
        for group in range(groups):
            for i in range(each):
                p = group * each + i
                for k, part in enumerate((1, 2)):
                    send[0, group, side, k * each + i : k * each + i + 1, :] = (
                        copied[p, part, row : row + 1, :] + jitter[p, part, row : row + 1, :]
                    )
    pl.semaphore_wait(barrier, 2)
    for side in (UP, DOWN):
        rim(side).start()
    for group in range(groups):
        for side in (UP, DOWN):
            swap(0, group, side).start()

    keep = 1.0 / (1.0 + DT * drag[...])
    flux_c[...] = 0.5 * DT * depth[...]
    keep_c[...] = keep
    turn_c[...] = DT * coriolis[...] * keep
    push_c[...] = 0.5 * DT * keep
    for p in range(members):
        out[p] = copied[p] + jitter[p]
    for side in (UP, DOWN):
        rim(side).wait_recv()
    edge = []
    for side in (UP, DOWN):
        k = 1.0 / (1.0 + DT * rim_recv[side, 2:3, :])
        edge.append(
            (0.5 * DT * rim_recv[side, 0:1, :], k, DT * rim_recv[side, 1:2, :] * k, 0.5 * DT * k)
        )
    for side in (UP, DOWN):
        for k in range(4):
            rim_recv[side, k : k + 1, :] = edge[side][k]

    def finish(step, group):
        for side in (UP, DOWN):
            swap(step, group, side).wait_recv()
        for i in range(each):
            p = group * each + i
            if step == STEPS:
                up, down = last_recv[group, UP, i : i + 1, :], last_recv[group, DOWN, i : i + 1, :]
            else:
                up, down = recv[step, group, UP, i : i + 1, :], recv[step, group, DOWN, i : i + 1, :]
            height = out[p, 0]
            out[p, 2] = out[p, 2] - push_c[...] * row_difference(height, up, down)
            if step == STEPS:
                continue
            for side, near, own in ((UP, up, height[0:1, :]), (DOWN, down, height[rows - 1 : rows, :])):
                far = recv[step, group, side, each + i : each + i + 1, :]
                k, t, b = (rim_recv[side, n : n + 1, :] for n in (1, 2, 3))
                u, v = halo[p, side, 0:1, :], halo[p, side, 1:2, :]
                across = own - far if side == UP else far - own
                halo[p, side, 0:1, :] = u * k + t * v - b * column_difference(near, True)
                halo[p, side, 1:2, :] = v * k - t * u - b * across

    for step in range(1, STEPS + 1):
        for group in range(groups):
            if step == 1:
                for side in (UP, DOWN):
                    swap(0, group, side).wait_recv()
                for side in (UP, DOWN):
                    for i in range(each):
                        for k in range(2):
                            halo[group * each + i, side, k : k + 1, :] = recv[
                                0, group, side, k * each + i : k * each + i + 1, :
                            ]
            else:
                finish(step - 1, group)
            for i in range(each):
                p = group * each + i
                u, v = out[p, 1], out[p, 2]
                f = flux_c[...]
                height = out[p, 0] - (
                    column_difference(f * u, False)
                    + row_difference(
                        f * v,
                        rim_recv[UP, 0:1, :] * halo[p, UP, 1:2, :],
                        rim_recv[DOWN, 0:1, :] * halo[p, DOWN, 1:2, :],
                    )
                )
                out[p, 0] = height
                if step == STEPS:
                    last_send[group, UP, i : i + 1, :] = height[0:1, :]
                    last_send[group, DOWN, i : i + 1, :] = height[rows - 1 : rows, :]
                else:
                    for k in range(2):
                        at = slice(k * each + i, k * each + i + 1)
                        send[step, group, UP, at, :] = height[k : k + 1, :]
                        send[step, group, DOWN, at, :] = height[rows - 1 - k : rows - k, :]
            for side in (UP, DOWN):
                swap(step, group, side).start()
            for i in range(each):
                p = group * each + i
                u, v = out[p, 1], out[p, 2]
                out[p, 1] = u * keep_c[...] + turn_c[...] * v - push_c[...] * column_difference(out[p, 0], True)
                out[p, 2] = v * keep_c[...] - turn_c[...] * u
    for group in range(groups):
        finish(STEPS, group)
    for side in (UP, DOWN):
        rim(side).wait_send()
        for step in range(STEPS + 1):
            for group in range(groups):
                swap(step, group, side).wait_send()


def advance(copied, jitter, depth, coriolis, drag, count):
    members, _, rows, width = jitter.shape
    groups = 2
    each = members // groups
    f32 = jnp.float32
    plane = pltpu.VMEM((rows, width), f32)
    copies = 1 + (STEPS + 1) * groups
    return pl.pallas_call(
        functools.partial(advance_kernel, count, groups),
        out_shape=jax.ShapeDtypeStruct(jitter.shape, f32),
        in_specs=[pl.BlockSpec(memory_space=pltpu.VMEM)] * 5,
        out_specs=pl.BlockSpec(memory_space=pltpu.VMEM),
        scratch_shapes=[
            plane, plane, plane, plane,
            pltpu.VMEM((2, 4, width), f32),
            pltpu.VMEM((2, 4, width), f32),
            pltpu.VMEM((STEPS, groups, 2, 2 * each, width), f32),
            pltpu.VMEM((STEPS, groups, 2, 2 * each, width), f32),
            pltpu.VMEM((groups, 2, each, width), f32),
            pltpu.VMEM((groups, 2, each, width), f32),
            pltpu.VMEM((members, 2, 2, width), f32),
            pltpu.SemaphoreType.DMA((copies, 2)),
            pltpu.SemaphoreType.DMA((copies, 2)),
        ],
        compiler_params=pltpu.CompilerParams(
            collective_id=0, has_side_effects=True, vmem_limit_bytes=40 * 1024 * 1024
        ),
        name="advance",
    )(copied, jitter, depth, coriolis, drag)


def local(count, ancestor, state, jitter, depth, coriolis, drag):
    members = state.shape[0]
    part = ancestor.shape[0]
    first = lax.axis_index("dom") * members
    index = jnp.arange(part, dtype=jnp.int32)
    moved = ancestor != index
    donor = jnp.any((ancestor[:, None] == index[None, :]) & moved[:, None], axis=0)
    earlier = (index[None, :] < index[:, None]) & (index[None, :] // members == index[:, None] // members)
    place = jnp.sum((earlier & donor[None, :]).astype(jnp.int32), axis=1)
    sent = []
    for k in range(CAP):
        hit = donor & (place == k) & (index // members == first // members)
        slot = jnp.sum(jnp.where(hit, index - first, 0))
        sent.append(lax.dynamic_slice_in_dim(state, slot, 1))
    pool = lax.all_gather(jnp.concatenate(sent), "dom", axis=0, tiled=True)
    where = (ancestor // members) * CAP + jnp.sum(
        jnp.where(ancestor[:, None] == index[None, :], place[None, :], 0), axis=1
    )
    copied = []
    for k in range(members):
        j = first + k
        got = lax.dynamic_slice_in_dim(pool, where[j], 1)
        copied.append(jnp.where(moved[j], got, state[k : k + 1]))
    return advance(jnp.concatenate(copied), jitter, depth, coriolis, drag, count)


def solution(mesh):
    field = P("dom", None, "space", None)
    plane = P("space", None)
    return jax.shard_map(
        functools.partial(local, mesh.shape["space"]),
        mesh=mesh,
        in_specs=(P(), field, field, plane, plane, plane),
        out_specs=field,
        check_vma=False,
    )
```

```python
import functools

import jax
import jax.numpy as jnp
from jax import lax
from jax.experimental import pallas as pl
from jax.experimental.pallas import tpu as pltpu
from jax.sharding import PartitionSpec as P

STEPS = 4
DT = 0.3
CAP = 2
MESH = pl.DeviceIdType.MESH
UP, DOWN = 0, 1


def column_difference(a, edge):
    width = a.shape[1]
    column = lax.broadcasted_iota(jnp.int32, a.shape, 1)
    beyond = a if edge else jnp.zeros_like(a)
    after = jnp.where(column == width - 1, beyond, pltpu.roll(a, width - 1, 1))
    before = jnp.where(column == 0, beyond, pltpu.roll(a, 1, 1))
    return after - before


def row_difference(a, above, below):
    rows = a.shape[0]
    row = lax.broadcasted_iota(jnp.int32, a.shape, 0)
    after = jnp.where(row == rows - 1, below, pltpu.roll(a, rows - 1, 0))
    before = jnp.where(row == 0, above, pltpu.roll(a, 1, 0))
    return after - before


def advance_kernel(
    count, groups,
    fields, depth, coriolis, drag, out,
    flux_c, keep_c, turn_c, push_c, rim_send, rim_recv, send, recv, last_send, last_recv, halo,
    send_sem, recv_sem,
):
    members, _, rows, width = out.shape
    each = members // groups
    me = lax.axis_index("space")
    above, below = lax.rem(me + count - 1, count), lax.rem(me + 1, count)
    towards = (above, below)

    barrier = pltpu.get_barrier_semaphore()
    for neighbour in towards:
        pl.semaphore_signal(barrier, inc=1, device_id={"space": neighbour}, device_id_type=MESH)

    def exchange(number, source, target, side):
        return pltpu.make_async_remote_copy(
            src_ref=source, dst_ref=target,
            send_sem=send_sem.at[number, side], recv_sem=recv_sem.at[number, 1 - side],
            device_id={"space": towards[side]}, device_id_type=MESH,
        )

    def rim(side):
        return exchange(0, rim_send.at[side], rim_recv.at[1 - side], side)

    def swap(step, group, side):
        number = 1 + step * groups + group
        if step == STEPS:
            return exchange(number, last_send.at[group, side], last_recv.at[group, 1 - side], side)
        return exchange(number, send.at[step, group, side], recv.at[step, group, 1 - side], side)

    for side, row in ((UP, 0), (DOWN, rows - 1)):
        for k, plane in enumerate((depth, coriolis, drag, drag)):
            rim_send[side, k : k + 1, :] = plane[row : row + 1, :]
        for group in range(groups):
            for i in range(each):
                p = group * each + i
                for k, part in enumerate((1, 2)):
                    send[0, group, side, k * each + i : k * each + i + 1, :] = fields[
                        p, part, row : row + 1, :
                    ]
    pl.semaphore_wait(barrier, 2)
    for side in (UP, DOWN):
        rim(side).start()
    for group in range(groups):
        for side in (UP, DOWN):
            swap(0, group, side).start()

    keep = 1.0 / (1.0 + DT * drag[...])
    flux_c[...] = 0.5 * DT * depth[...]
    keep_c[...] = keep
    turn_c[...] = DT * coriolis[...] * keep
    push_c[...] = 0.5 * DT * keep
    for p in range(members):
        out[p] = fields[p]
    for side in (UP, DOWN):
        rim(side).wait_recv()
    edge = []
    for side in (UP, DOWN):
        k = 1.0 / (1.0 + DT * rim_recv[side, 2:3, :])
        edge.append(
            (0.5 * DT * rim_recv[side, 0:1, :], k, DT * rim_recv[side, 1:2, :] * k, 0.5 * DT * k)
        )
    for side in (UP, DOWN):
        for k in range(4):
            rim_recv[side, k : k + 1, :] = edge[side][k]

    def finish(step, group):
        for side in (UP, DOWN):
            swap(step, group, side).wait_recv()
        for i in range(each):
            p = group * each + i
            if step == STEPS:
                up, down = last_recv[group, UP, i : i + 1, :], last_recv[group, DOWN, i : i + 1, :]
            else:
                up, down = recv[step, group, UP, i : i + 1, :], recv[step, group, DOWN, i : i + 1, :]
            height = out[p, 0]
            out[p, 2] = out[p, 2] - push_c[...] * row_difference(height, up, down)
            if step == STEPS:
                continue
            for side, near, own in ((UP, up, height[0:1, :]), (DOWN, down, height[rows - 1 : rows, :])):
                far = recv[step, group, side, each + i : each + i + 1, :]
                k, t, b = (rim_recv[side, n : n + 1, :] for n in (1, 2, 3))
                u, v = halo[p, side, 0:1, :], halo[p, side, 1:2, :]
                across = own - far if side == UP else far - own
                halo[p, side, 0:1, :] = u * k + t * v - b * column_difference(near, True)
                halo[p, side, 1:2, :] = v * k - t * u - b * across

    for step in range(1, STEPS + 1):
        for group in range(groups):
            if step == 1:
                for side in (UP, DOWN):
                    swap(0, group, side).wait_recv()
                for side in (UP, DOWN):
                    for i in range(each):
                        for k in range(2):
                            halo[group * each + i, side, k : k + 1, :] = recv[
                                0, group, side, k * each + i : k * each + i + 1, :
                            ]
            else:
                finish(step - 1, group)
            for i in range(each):
                p = group * each + i
                u, v = out[p, 1], out[p, 2]
                f = flux_c[...]
                height = out[p, 0] - (
                    column_difference(f * u, False)
                    + row_difference(
                        f * v,
                        rim_recv[UP, 0:1, :] * halo[p, UP, 1:2, :],
                        rim_recv[DOWN, 0:1, :] * halo[p, DOWN, 1:2, :],
                    )
                )
                out[p, 0] = height
                if step == STEPS:
                    last_send[group, UP, i : i + 1, :] = height[0:1, :]
                    last_send[group, DOWN, i : i + 1, :] = height[rows - 1 : rows, :]
                else:
                    for k in range(2):
                        at = slice(k * each + i, k * each + i + 1)
                        send[step, group, UP, at, :] = height[k : k + 1, :]
                        send[step, group, DOWN, at, :] = height[rows - 1 - k : rows - k, :]
            for side in (UP, DOWN):
                swap(step, group, side).start()
            for i in range(each):
                p = group * each + i
                u, v = out[p, 1], out[p, 2]
                out[p, 1] = u * keep_c[...] + turn_c[...] * v - push_c[...] * column_difference(out[p, 0], True)
                out[p, 2] = v * keep_c[...] - turn_c[...] * u
    for group in range(groups):
        finish(STEPS, group)
    for side in (UP, DOWN):
        rim(side).wait_send()
        for step in range(STEPS + 1):
            for group in range(groups):
                swap(step, group, side).wait_send()


def advance(fields, depth, coriolis, drag, count):
    members, _, rows, width = fields.shape
    groups = 2
    each = members // groups
    f32 = jnp.float32
    plane = pltpu.VMEM((rows, width), f32)
    copies = 1 + (STEPS + 1) * groups
    return pl.pallas_call(
        functools.partial(advance_kernel, count, groups),
        out_shape=jax.ShapeDtypeStruct(fields.shape, f32),
        in_specs=[pl.BlockSpec(memory_space=pltpu.VMEM)] * 4,
        out_specs=pl.BlockSpec(memory_space=pltpu.VMEM),
        scratch_shapes=[
            plane, plane, plane, plane,
            pltpu.VMEM((2, 4, width), f32),
            pltpu.VMEM((2, 4, width), f32),
            pltpu.VMEM((STEPS, groups, 2, 2 * each, width), f32),
            pltpu.VMEM((STEPS, groups, 2, 2 * each, width), f32),
            pltpu.VMEM((groups, 2, each, width), f32),
            pltpu.VMEM((groups, 2, each, width), f32),
            pltpu.VMEM((members, 2, 2, width), f32),
            pltpu.SemaphoreType.DMA((copies, 2)),
            pltpu.SemaphoreType.DMA((copies, 2)),
        ],
        compiler_params=pltpu.CompilerParams(
            collective_id=0, has_side_effects=True, vmem_limit_bytes=40 * 1024 * 1024
        ),
        name="advance",
    )(fields, depth, coriolis, drag)


def routes_kernel(members, across, down, out):
    part = across.shape[1]
    me = lax.axis_index("dom")
    chip = me // 2
    lane = lax.broadcasted_iota(jnp.int32, (part, part), 1)
    sub = lax.broadcasted_iota(jnp.int32, (part, part), 0)
    row_p, col_p = lane[0:1, :], sub[:, 0:1]

    def over(mask, value, axis):
        return jnp.sum(jnp.where(mask, value, 0), axis=axis, keepdims=True)

    target_row = over((down[...] == lane) & (sub != lane), sub + 1, 0) - 1
    target_col = over((across[...] == sub) & (sub != lane), lane + 1, 1) - 1

    def chip_of(p):
        return lax.shift_right_arithmetic(p, (2 * members).bit_length() - 1)

    def block_of(p):
        return lax.shift_right_arithmetic(p, members.bit_length() - 1)

    d_row = jnp.where(target_row >= 0, chip_of(row_p) ^ chip_of(target_row), 0)
    d_col = jnp.where(target_col >= 0, chip_of(col_p) ^ chip_of(target_col), 0)
    rank = over((target_col >= 0) & (sub < lane) & (block_of(sub) == block_of(lane)), 1, 0)
    own = (block_of(row_p) & 1) * CAP + rank

    columns = [None] * 8
    most_first, most_second = jnp.int32(0), jnp.int32(0)
    for q in range(2):
        first, second = 1 + q, 2 - q
        f_row, f_col = (d_row & first) != 0, (d_col & first) != 0
        g_row, g_col = (d_row & second) != 0, (d_col & second) != 0
        s1 = over(f_col & (chip_of(sub) == chip_of(lane)) & (sub < lane), 1, 0)
        e_row = chip_of(row_p) ^ (d_row & first)
        e_col = chip_of(col_p) ^ (d_col & first)
        key_row = row_p + jnp.where(f_row, part, 0)
        key_col = col_p + jnp.where(f_col, part, 0)
        s2 = over(g_col & (e_col == e_row) & (key_col < key_row), 1, 0)
        found = jnp.where(g_row, 4 * CAP + s2, jnp.where(f_row, 2 * CAP + s1, own))
        columns[q] = over((s1 == sub) & f_row & (chip_of(row_p) == chip), own, 1)
        columns[2 + q] = over(
            (s2 == sub) & g_row & (e_row == chip), jnp.where(f_row, 2 * CAP + s1, own), 1
        )
        columns[4 + q] = over(target_row == sub, found, 1)
        most_first = jnp.maximum(most_first, jnp.max(jnp.where(f_row, s1 + 1, 0)))
        most_second = jnp.maximum(most_second, jnp.max(jnp.where(g_row, s2 + 1, 0)))
    columns[6] = jnp.where(down[...] != col_p, 1, 0)
    tier = jnp.int32(len(TIERS))
    for n in range(len(TIERS) - 1, -1, -1):
        fits = (most_first <= TIERS[n][0]) & (most_second <= TIERS[n][1])
        tier = jnp.where(fits, n, tier)
    mine = over((rank == sub) & (target_row >= 0) & (block_of(row_p) == me), row_p & (members - 1), 1)
    columns[7] = jnp.where(col_p < CAP, mine, tier)
    for k in range(8):
        out[:, k : k + 1] = columns[k]


TIERS = ((2, 2), (3, 3))


def resample_kernel(
    c1, c2,
    table, state, jitter, out,
    own0, own1, first_send0, first_send1, first_recv0, first_recv1,
    second_send0, second_send1, second_recv0, second_recv1, core_send, last_send, last_recv,
    send_sem, recv_sem,
):
    members, _, rows, width = out.shape
    half, wide = rows // 2, width // 2
    me = lax.axis_index("dom")
    core = lax.rem(me, 2)
    chip = me // 2
    other = me + 1 - 2 * core
    turned = (me + 2 - 4 * lax.rem(chip, 2), me + 4 - 8 * (chip // 2))
    own, first_send, first_recv = (own0, own1), (first_send0, first_send1), (first_recv0, first_recv1)
    second_send, second_recv = (second_send0, second_send1), (second_recv0, second_recv1)
    mine, theirs = pl.multiple_of(core * half, half), pl.multiple_of((1 - core) * half, half)

    barrier = pltpu.get_barrier_semaphore()
    for device in (other,) + turned:
        pl.semaphore_signal(barrier, inc=1, device_id={"dom": device}, device_id_type=MESH)

    def send(number, source, target, device):
        return pltpu.make_async_remote_copy(
            src_ref=source, dst_ref=target, send_sem=send_sem.at[number], recv_sem=recv_sem.at[number],
            device_id={"dom": device}, device_id_type=MESH,
        )

    cores = [
        send(q, core_send.at[q], own[q].at[pl.ds(core * CAP, CAP)], other) for q in range(2)
    ]
    firsts = [send(2 + q, first_send[q], first_recv[q], turned[q]) for q in range(2)]
    seconds = [send(4 + q, second_send[q], second_recv[q], turned[1 - q]) for q in range(2)]
    last = send(6, last_send, last_recv, other)

    for k in range(CAP):
        slot = table[k, 7]
        for q in range(2):
            columns = pl.ds(q * wide, wide)
            core_send[q, k] = state[slot, :, pl.ds(theirs, half), columns]
            own[q][core * CAP + k] = state[slot, :, pl.ds(mine, half), columns]
    pl.semaphore_wait(barrier, 3)
    for copy in cores:
        copy.start()
    for copy in cores:
        copy.wait_recv()
    for q in range(2):
        for k in range(c1):
            first_send[q][k] = own[q][table[k, q]]
        firsts[q].start()

    def pick(q, index, come):
        value = own[q][jnp.clip(index, 0, 2 * CAP - 1)]
        value = jnp.where(index >= 2 * CAP, first_recv[q][jnp.clip(index - 2 * CAP, 0, c1 - 1)], value)
        if come:
            value = jnp.where(
                index >= 4 * CAP, second_recv[q][jnp.clip(index - 4 * CAP, 0, c2 - 1)], value
            )
        return value

    for q in range(2):
        firsts[q].wait_recv()
        for k in range(c2):
            second_send[q][k] = pick(q, table[k, 2 + q], False)
        seconds[q].start()
    for q in range(2):
        seconds[q].wait_recv()
    for k in range(members):
        for q in range(2):
            last_send[k, :, :, q * wide : (q + 1) * wide] = pick(q, table[other * members + k, 4 + q], True)
    last.start()
    for k in range(members):
        moved = table[me * members + k, 6]
        for q in range(2):
            columns = pl.ds(q * wide, wide)
            got = pick(q, table[me * members + k, 4 + q], True)
            kept = state[k, :, pl.ds(mine, half), columns]
            out[k, :, pl.ds(mine, half), columns] = (
                jnp.where(moved != 0, got, kept) + jitter[k, :, pl.ds(mine, half), columns]
            )
    last.wait_recv()
    for k in range(members):
        moved = table[me * members + k, 6]
        kept = state[k, :, pl.ds(theirs, half), :]
        out[k, :, pl.ds(theirs, half), :] = (
            jnp.where(moved != 0, last_recv[k], kept) + jitter[k, :, pl.ds(theirs, half), :]
        )
    for copy in cores + firsts + seconds + [last]:
        copy.wait_send()


def resample(number, c1, c2, table, state, jitter):
    members, parts, rows, width = state.shape
    f32 = jnp.float32

    def slots(n, wide=width // 2):
        return pltpu.VMEM((n, parts, rows // 2, wide), f32)

    return pl.pallas_call(
        functools.partial(resample_kernel, c1, c2),
        out_shape=jax.ShapeDtypeStruct(state.shape, f32),
        in_specs=[pl.BlockSpec(memory_space=pltpu.SMEM)] + [pl.BlockSpec(memory_space=pltpu.VMEM)] * 2,
        out_specs=pl.BlockSpec(memory_space=pltpu.VMEM),
        scratch_shapes=[slots(2 * CAP)] * 2
        + [slots(c1)] * 4
        + [slots(c2)] * 4
        + [pltpu.VMEM((2, CAP, parts, rows // 2, width // 2), f32), slots(members, width), slots(members, width)]
        + [pltpu.SemaphoreType.DMA((7,))] * 2,
        compiler_params=pltpu.CompilerParams(
            collective_id=number, has_side_effects=True, vmem_limit_bytes=40 * 1024 * 1024
        ),
        name="resample",
    )(table, state, jitter)


def routed(ancestor, state, jitter):
    members = state.shape[0]
    part = ancestor.shape[0]
    table = pl.pallas_call(
        functools.partial(routes_kernel, members),
        out_shape=jax.ShapeDtypeStruct((part, 8), jnp.int32),
        in_specs=[pl.BlockSpec(memory_space=pltpu.VMEM)] * 2,
        out_specs=pl.BlockSpec(memory_space=pltpu.VMEM),
        name="routes",
    )(ancestor[None, :], ancestor[:, None])
    sizes = TIERS + ((2 * CAP, 2 * members),)
    return lax.switch(
        table[CAP, 7],
        [functools.partial(resample, 1 + n, c1, c2) for n, (c1, c2) in enumerate(sizes)],
        table, state, jitter,
    )


def gathered(ancestor, state, jitter):
    members = state.shape[0]
    part = ancestor.shape[0]
    first = lax.axis_index("dom") * members
    index = jnp.arange(part, dtype=jnp.int32)
    moved = ancestor != index
    donor = jnp.any((ancestor[:, None] == index[None, :]) & moved[:, None], axis=0)
    earlier = (index[None, :] < index[:, None]) & (index[None, :] // members == index[:, None] // members)
    place = jnp.sum((earlier & donor[None, :]).astype(jnp.int32), axis=1)
    sent = []
    for k in range(CAP):
        hit = donor & (place == k) & (index // members == first // members)
        slot = jnp.sum(jnp.where(hit, index - first, 0))
        sent.append(lax.dynamic_slice_in_dim(state, slot, 1))
    pool = lax.all_gather(jnp.concatenate(sent), "dom", axis=0, tiled=True)
    where = (ancestor // members) * CAP + jnp.sum(
        jnp.where(ancestor[:, None] == index[None, :], place[None, :], 0), axis=1
    )
    copied = []
    for k in range(members):
        j = first + k
        got = lax.dynamic_slice_in_dim(pool, where[j], 1)
        copied.append(jnp.where(moved[j], got, state[k : k + 1]))
    return jnp.concatenate(copied) + jitter


def local(count, doms, ancestor, state, jitter, depth, coriolis, drag):
    members = state.shape[0]
    simple = doms == 8 and members == 4 and state.shape[2] % 16 == 0
    fields = (routed if simple else gathered)(ancestor, state, jitter)
    return advance(fields, depth, coriolis, drag, count)


def solution(mesh):
    field = P("dom", None, "space", None)
    plane = P("space", None)
    return jax.shard_map(
        functools.partial(local, mesh.shape["space"], mesh.shape["dom"]),
        mesh=mesh,
        in_specs=(P(), field, field, plane, plane, plane),
        out_specs=field,
        check_vma=False,
    )
```

```python
import functools

import jax
import jax.numpy as jnp
from jax import lax
from jax.experimental import pallas as pl
from jax.experimental.pallas import tpu as pltpu
from jax.sharding import PartitionSpec as P

STEPS = 4
DT = 0.3
CAP = 2
MESH = pl.DeviceIdType.MESH
UP, DOWN = 0, 1


def column_difference(a, edge):
    width = a.shape[1]
    column = lax.broadcasted_iota(jnp.int32, a.shape, 1)
    beyond = a if edge else jnp.zeros_like(a)
    after = jnp.where(column == width - 1, beyond, pltpu.roll(a, width - 1, 1))
    before = jnp.where(column == 0, beyond, pltpu.roll(a, 1, 1))
    return after - before


def row_difference(a, above, below):
    rows = a.shape[0]
    row = lax.broadcasted_iota(jnp.int32, a.shape, 0)
    after = jnp.where(row == rows - 1, below, pltpu.roll(a, rows - 1, 0))
    before = jnp.where(row == 0, above, pltpu.roll(a, 1, 0))
    return after - before


def exchange(axis, number, source, target, device, send_sem, recv_sem):
    return pltpu.make_async_remote_copy(
        src_ref=source, dst_ref=target, send_sem=send_sem.at[number], recv_sem=recv_sem.at[number],
        device_id={axis: device}, device_id_type=MESH,
    )


def advance_kernel(
    count, groups,
    fields, depth, coriolis, drag, rim, out,
    flux_c, keep_c, turn_c, push_c, rim_c, send, recv, last_send, last_recv, halo, near, far,
    send_sem, recv_sem,
):
    members, _, rows, width = out.shape
    each = members // groups
    me = lax.axis_index("space")
    towards = (lax.rem(me + count - 1, count), lax.rem(me + 1, count))

    barrier = pltpu.get_barrier_semaphore()
    for neighbour in towards:
        pl.semaphore_signal(barrier, inc=1, device_id={"space": neighbour}, device_id_type=MESH)

    def swap(step, group, side):
        number = 2 * (step * groups + group) + side
        if step == STEPS:
            source, target = last_send.at[group, side], last_recv.at[group, 1 - side]
        else:
            source, target = send.at[step, group, side], recv.at[step, group, 1 - side]
        return exchange("space", number, source, target, towards[side], send_sem, recv_sem)

    for group in range(groups):
        for side, row in ((UP, 0), (DOWN, rows - 1)):
            for i in range(each):
                for k in range(2):
                    at = slice(k * each + i, k * each + i + 1)
                    send[0, group, side, at, :] = fields[group * each + i, 1 + k, row : row + 1, :]
    pl.semaphore_wait(barrier, 2)
    for group in range(groups):
        for side in (UP, DOWN):
            swap(0, group, side).start()

    keep = 1.0 / (1.0 + DT * drag[...])
    flux_c[...] = 0.5 * DT * depth[...]
    keep_c[...] = keep
    turn_c[...] = DT * coriolis[...] * keep
    push_c[...] = 0.5 * DT * keep
    for side in (UP, DOWN):
        rim_depth, rim_coriolis, rim_drag = (rim[side, k : k + 1, :] for k in range(3))
        k = 1.0 / (1.0 + DT * rim_drag)
        for i in range(each):
            at = slice(side * each + i, side * each + i + 1)
            rim_c[0, at, :] = 0.5 * DT * rim_depth
            rim_c[1, at, :] = k
            rim_c[2, at, :] = DT * rim_coriolis * k
            rim_c[3, at, :] = 0.5 * DT * k
            rim_c[4, at, :] = 0.5 * DT * k if side == UP else -0.5 * DT * k

    def finish(step, group):
        for side in (UP, DOWN):
            swap(step, group, side).wait_recv()
        come = last_recv.at[group] if step == STEPS else recv.at[step, group]
        if step < STEPS:
            for side in (UP, DOWN):
                at = slice(side * each, (side + 1) * each)
                near[at, :] = come[side, 0:each, :]
                far[at, :] = send[step, group, side, 0:each, :] - come[side, each : 2 * each, :]
            u, v = halo[group, 0], halo[group, 1]
            halo[group, 0] = u * rim_c[1] + v * rim_c[2] - rim_c[3] * column_difference(near[...], True)
            halo[group, 1] = v * rim_c[1] - u * rim_c[2] - rim_c[4] * far[...]
        for i in range(each):
            p = group * each + i
            out[p, 2] = out[p, 2] - push_c[...] * row_difference(
                out[p, 0], come[UP, i : i + 1, :], come[DOWN, i : i + 1, :]
            )

    for step in range(1, STEPS + 1):
        old = fields if step == 1 else out
        for group in range(groups):
            if step == 1:
                for side in (UP, DOWN):
                    swap(0, group, side).wait_recv()
                for side in (UP, DOWN):
                    for k in range(2):
                        halo[group, k, side * each : (side + 1) * each, :] = recv[
                            0, group, side, k * each : (k + 1) * each, :
                        ]
            else:
                finish(step - 1, group)
            near[...] = rim_c[0] * halo[group, 1]
            for i in range(each):
                p = group * each + i
                f = flux_c[...]
                height = old[p, 0] - (
                    column_difference(f * old[p, 1], False)
                    + row_difference(f * old[p, 2], near[i : i + 1, :], near[each + i : each + i + 1, :])
                )
                out[p, 0] = height
                if step == STEPS:
                    last_send[group, UP, i : i + 1, :] = height[0:1, :]
                    last_send[group, DOWN, i : i + 1, :] = height[rows - 1 : rows, :]
                else:
                    for k in range(2):
                        at = slice(k * each + i, k * each + i + 1)
                        send[step, group, UP, at, :] = height[k : k + 1, :]
                        send[step, group, DOWN, at, :] = height[rows - 1 - k : rows - k, :]
            for side in (UP, DOWN):
                swap(step, group, side).start()
            for i in range(each):
                p = group * each + i
                u, v = old[p, 1], old[p, 2]
                out[p, 1] = u * keep_c[...] + turn_c[...] * v - push_c[...] * column_difference(out[p, 0], True)
                out[p, 2] = v * keep_c[...] - turn_c[...] * u
    for group in range(groups):
        finish(STEPS, group)
    for step in range(STEPS + 1):
        for group in range(groups):
            for side in (UP, DOWN):
                swap(step, group, side).wait_send()


def advance(fields, depth, coriolis, drag, rim, count):
    members, _, rows, width = fields.shape
    groups = 2
    each = members // groups
    f32 = jnp.float32
    plane = pltpu.VMEM((rows, width), f32)
    edges = pltpu.VMEM((2 * each, width), f32)
    copies = 2 * (STEPS + 1) * groups
    return pl.pallas_call(
        functools.partial(advance_kernel, count, groups),
        out_shape=jax.ShapeDtypeStruct(fields.shape, f32),
        in_specs=[pl.BlockSpec(memory_space=pltpu.VMEM)] * 5,
        out_specs=pl.BlockSpec(memory_space=pltpu.VMEM),
        scratch_shapes=[
            plane, plane, plane, plane,
            pltpu.VMEM((5, 2 * each, width), f32),
            pltpu.VMEM((STEPS, groups, 2, 2 * each, width), f32),
            pltpu.VMEM((STEPS, groups, 2, 2 * each, width), f32),
            pltpu.VMEM((groups, 2, each, width), f32),
            pltpu.VMEM((groups, 2, each, width), f32),
            pltpu.VMEM((groups, 2, 2 * each, width), f32),
            edges, edges,
            pltpu.SemaphoreType.DMA((copies,)),
            pltpu.SemaphoreType.DMA((copies,)),
        ],
        compiler_params=pltpu.CompilerParams(
            collective_id=0, has_side_effects=True, vmem_limit_bytes=40 * 1024 * 1024
        ),
        name="advance",
    )(fields, depth, coriolis, drag, rim)


def routes_kernel(members, across, out, tier_out):
    part = across.shape[1]
    me = lax.axis_index("dom")
    chip = me // 2
    lane = lax.broadcasted_iota(jnp.int32, (part, part), 1)
    sub = lax.broadcasted_iota(jnp.int32, (part, part), 0)
    row_p, col_p = lane[0:1, :], sub[:, 0:1]
    down = jnp.sum(jnp.where(lane == sub, across[...], 0), axis=1, keepdims=True)

    def over(mask, value, axis):
        return jnp.sum(jnp.where(mask, value, 0), axis=axis, keepdims=True)

    target_row = over((down == lane) & (sub != lane), sub + 1, 0) - 1
    target_col = over((across[...] == sub) & (sub != lane), lane + 1, 1) - 1

    def chip_of(p):
        return lax.shift_right_arithmetic(p, (2 * members).bit_length() - 1)

    def block_of(p):
        return lax.shift_right_arithmetic(p, members.bit_length() - 1)

    d_row = jnp.where(target_row >= 0, chip_of(row_p) ^ chip_of(target_row), 0)
    d_col = jnp.where(target_col >= 0, chip_of(col_p) ^ chip_of(target_col), 0)
    rank = over((target_col >= 0) & (sub < lane) & (block_of(sub) == block_of(lane)), 1, 0)
    own = (block_of(row_p) & 1) * CAP + rank

    columns = [None] * 8
    most_first, most_second = jnp.int32(0), jnp.int32(0)
    for q in range(2):
        first, second = 1 + q, 2 - q
        f_row, f_col = (d_row & first) != 0, (d_col & first) != 0
        g_row, g_col = (d_row & second) != 0, (d_col & second) != 0
        s1 = over(f_col & (chip_of(sub) == chip_of(lane)) & (sub < lane), 1, 0)
        e_row = chip_of(row_p) ^ (d_row & first)
        e_col = chip_of(col_p) ^ (d_col & first)
        key_row = row_p + jnp.where(f_row, part, 0)
        key_col = col_p + jnp.where(f_col, part, 0)
        s2 = over(g_col & (e_col == e_row) & (key_col < key_row), 1, 0)
        found = jnp.where(g_row, 4 * CAP + s2, jnp.where(f_row, 2 * CAP + s1, own))
        columns[q] = over((s1 == sub) & f_row & (chip_of(row_p) == chip), own, 1)
        columns[2 + q] = over(
            (s2 == sub) & g_row & (e_row == chip), jnp.where(f_row, 2 * CAP + s1, own), 1
        )
        columns[4 + q] = over(target_row == sub, found, 1)
        most_first = jnp.maximum(most_first, jnp.max(jnp.where(f_row, s1 + 1, 0)))
        most_second = jnp.maximum(most_second, jnp.max(jnp.where(g_row, s2 + 1, 0)))
    columns[6] = jnp.where(down != col_p, 1, 0)
    tier = jnp.int32(len(TIERS))
    for n in range(len(TIERS) - 1, -1, -1):
        fits = (most_first <= TIERS[n][0]) & (most_second <= TIERS[n][1])
        tier = jnp.where(fits, n, tier)
    mine = over((rank == sub) & (target_row >= 0) & (block_of(row_p) == me), row_p & (members - 1), 1)
    columns[7] = mine
    tier_out[0] = tier
    for k in range(8):
        out[:, k : k + 1] = columns[k]


TIERS = ((2, 2), (3, 3), (4, 4))
PIECES = 4


def resample_kernel(
    c1, c2, count,
    table, state, jitter, depth, coriolis, drag, out, rim,
    rim_send, core_send, last_send, last_recv, own_all, first_send_all, first_recv_all, second_send_all, second_recv_all,
    send_sem, recv_sem, rim_send_sem, rim_recv_sem,
):
    members, _, rows, width = out.shape
    half, wide = rows // 2, width // PIECES
    pieces = range(PIECES)
    me = lax.axis_index("dom")
    core = lax.rem(me, 2)
    chip = me // 2
    other = me + 1 - 2 * core
    turned = (me + 2 - 4 * lax.rem(chip, 2), me + 4 - 8 * (chip // 2))
    slab = lax.axis_index("space")
    towards = (lax.rem(slab + count - 1, count), lax.rem(slab + 1, count))
    mine, theirs = pl.multiple_of(core * half, half), pl.multiple_of((1 - core) * half, half)

    barrier = pltpu.get_barrier_semaphore()
    for device in (other,) + turned:
        pl.semaphore_signal(barrier, inc=1, device_id={"dom": device}, device_id_type=MESH)
    for neighbour in towards:
        pl.semaphore_signal(barrier, inc=1, device_id={"space": neighbour}, device_id_type=MESH)

    def send(number, source, target, device):
        return exchange("dom", number, source, target, device, send_sem, recv_sem)

    rims = [
        exchange("space", side, rim_send.at[side], rim.at[1 - side], towards[side], rim_send_sem, rim_recv_sem)
        for side in (UP, DOWN)
    ]
    own, first_send, first_recv, second_send, second_recv = (
        tuple(ref for ref in refs) for refs in
        (own_all, first_send_all, first_recv_all, second_send_all, second_recv_all)
    )
    cores = [send(t, core_send.at[t], own[t].at[pl.ds(core * CAP, CAP)], other) for t in pieces]
    firsts = [send(PIECES + t, first_send[t], first_recv[t], turned[t % 2]) for t in pieces]
    seconds = [send(2 * PIECES + t, second_send[t], second_recv[t], turned[1 - t % 2]) for t in pieces]
    lasts = [send(3 * PIECES + t, last_send.at[t], last_recv.at[t], other) for t in pieces]

    for side, row in ((UP, 0), (DOWN, rows - 1)):
        for k, plane in enumerate((depth, coriolis, drag, drag)):
            rim_send[side, k : k + 1, :] = plane[row : row + 1, :]
    for t in pieces:
        columns = pl.ds(t * wide, wide)
        for k in range(CAP):
            slot = table[k, 7]
            core_send[t, k] = state[slot, :, pl.ds(theirs, half), columns]
            own[t][core * CAP + k] = state[slot, :, pl.ds(mine, half), columns]
    pl.semaphore_wait(barrier, 5)
    for t in pieces:
        cores[t].start()
    for copy in rims:
        copy.start()
    for t in pieces:
        cores[t].wait_recv()
        for k in range(c1):
            first_send[t][k] = own[t][table[k, t % 2]]
        firsts[t].start()

    def pick(t, index, come):
        value = own[t][jnp.clip(index, 0, 2 * CAP - 1)]
        value = jnp.where(index >= 2 * CAP, first_recv[t][jnp.clip(index - 2 * CAP, 0, c1 - 1)], value)
        if come:
            value = jnp.where(
                index >= 4 * CAP, second_recv[t][jnp.clip(index - 4 * CAP, 0, c2 - 1)], value
            )
        return value

    for t in pieces:
        firsts[t].wait_recv()
        for k in range(c2):
            second_send[t][k] = pick(t, table[k, 2 + t % 2], False)
        seconds[t].start()
    for t in pieces:
        seconds[t].wait_recv()
        for k in range(members):
            last_send[t, k] = pick(t, table[other * members + k, 4 + t % 2], True)
        lasts[t].start()
        columns = pl.ds(t * wide, wide)
        for k in range(members):
            got = pick(t, table[me * members + k, 4 + t % 2], True)
            kept = state[k, :, pl.ds(mine, half), columns]
            out[k, :, pl.ds(mine, half), columns] = (
                jnp.where(table[me * members + k, 6] != 0, got, kept) + jitter[k, :, pl.ds(mine, half), columns]
            )
    for t in pieces:
        lasts[t].wait_recv()
        columns = pl.ds(t * wide, wide)
        for k in range(members):
            kept = state[k, :, pl.ds(theirs, half), columns]
            out[k, :, pl.ds(theirs, half), columns] = (
                jnp.where(table[me * members + k, 6] != 0, last_recv[t, k], kept)
                + jitter[k, :, pl.ds(theirs, half), columns]
            )
    for copy in rims:
        copy.wait()
    for copy in cores + firsts + seconds + lasts:
        copy.wait_send()


def resample(number, c1, c2, count, table, state, jitter, depth, coriolis, drag):
    members, parts, rows, width = state.shape
    f32 = jnp.float32
    vmem = pl.BlockSpec(memory_space=pltpu.VMEM)

    def slots(*lead):
        return pltpu.VMEM((*lead, parts, rows // 2, width // PIECES), f32)

    return pl.pallas_call(
        functools.partial(resample_kernel, c1, c2, count),
        out_shape=(
            jax.ShapeDtypeStruct(state.shape, f32), jax.ShapeDtypeStruct((2, 4, width), f32),
        ),
        in_specs=[pl.BlockSpec(memory_space=pltpu.SMEM)] + [vmem] * 5,
        out_specs=(vmem, vmem),
        scratch_shapes=[
            pltpu.VMEM((2, 4, width), f32),
            slots(PIECES, CAP), slots(PIECES, members), slots(PIECES, members),
            [slots(2 * CAP)] * PIECES, [slots(c1)] * PIECES, [slots(c1)] * PIECES,
            [slots(c2)] * PIECES, [slots(c2)] * PIECES,
            pltpu.SemaphoreType.DMA((4 * PIECES,)), pltpu.SemaphoreType.DMA((4 * PIECES,)),
            pltpu.SemaphoreType.DMA((2,)), pltpu.SemaphoreType.DMA((2,)),
        ],
        compiler_params=pltpu.CompilerParams(
            collective_id=number, has_side_effects=True, vmem_limit_bytes=40 * 1024 * 1024
        ),
        name="resample",
    )(table, state, jitter, depth, coriolis, drag)


def routed(count, ancestor, state, jitter, *planes):
    members = state.shape[0]
    part = ancestor.shape[0]
    table, tier = pl.pallas_call(
        functools.partial(routes_kernel, members),
        out_shape=(
            jax.ShapeDtypeStruct((part, 8), jnp.int32), jax.ShapeDtypeStruct((1,), jnp.int32),
        ),
        in_specs=[pl.BlockSpec(memory_space=pltpu.VMEM)],
        out_specs=(pl.BlockSpec(memory_space=pltpu.VMEM), pl.BlockSpec(memory_space=pltpu.SMEM)),
        name="routes",
    )(ancestor[None, :])
    sizes = TIERS + ((2 * CAP, 2 * members),)
    return lax.switch(
        tier[0],
        [functools.partial(resample, 1 + n, c1, c2, count) for n, (c1, c2) in enumerate(sizes)],
        table, state, jitter, *planes,
    )


def edge_rows(count, *planes):
    stacked = jnp.stack(planes + planes[-1:])
    after = [(i, (i + 1) % count) for i in range(count)]
    before = [((i + 1) % count, i) for i in range(count)]
    return jnp.stack(
        [lax.ppermute(stacked[:, -1], "space", after), lax.ppermute(stacked[:, 0], "space", before)]
    )


def gathered(ancestor, state, jitter):
    members = state.shape[0]
    part = ancestor.shape[0]
    first = lax.axis_index("dom") * members
    index = jnp.arange(part, dtype=jnp.int32)
    moved = ancestor != index
    donor = jnp.any((ancestor[:, None] == index[None, :]) & moved[:, None], axis=0)
    earlier = (index[None, :] < index[:, None]) & (index[None, :] // members == index[:, None] // members)
    place = jnp.sum((earlier & donor[None, :]).astype(jnp.int32), axis=1)
    sent = []
    for k in range(CAP):
        hit = donor & (place == k) & (index // members == first // members)
        slot = jnp.sum(jnp.where(hit, index - first, 0))
        sent.append(lax.dynamic_slice_in_dim(state, slot, 1))
    pool = lax.all_gather(jnp.concatenate(sent), "dom", axis=0, tiled=True)
    where = (ancestor // members) * CAP + jnp.sum(
        jnp.where(ancestor[:, None] == index[None, :], place[None, :], 0), axis=1
    )
    copied = []
    for k in range(members):
        j = first + k
        got = lax.dynamic_slice_in_dim(pool, where[j], 1)
        copied.append(jnp.where(moved[j], got, state[k : k + 1]))
    return jnp.concatenate(copied) + jitter


def local(count, doms, ancestor, state, jitter, depth, coriolis, drag):
    members = state.shape[0]
    simple = doms == 8 and members == 4 and state.shape[2] % 16 == 0
    planes = (depth, coriolis, drag)
    if simple:
        fields, rim = routed(count, ancestor, state, jitter, *planes)
    else:
        fields, rim = gathered(ancestor, state, jitter), edge_rows(count, *planes)
    return advance(fields, *planes, rim, count)


def solution(mesh):
    field = P("dom", None, "space", None)
    plane = P("space", None)
    return jax.shard_map(
        functools.partial(local, mesh.shape["space"], mesh.shape["dom"]),
        mesh=mesh,
        in_specs=(P(), field, field, plane, plane, plane),
        out_specs=field,
        check_vma=False,
    )
```

```python
import functools

import jax
import jax.numpy as jnp
from jax import lax
from jax.experimental import pallas as pl
from jax.experimental.pallas import tpu as pltpu
from jax.sharding import PartitionSpec as P

STEPS = 4
DT = 0.3
CAP = 2
MESH = pl.DeviceIdType.MESH
UP, DOWN = 0, 1


def column_difference(load, start, size, width, edge):
    low, high = max(start - 128, 0), min(start + size + 128, width)
    a = load(low, high)
    after = pltpu.roll(a, high - low - 1, 1)[:, start - low : start - low + size]
    before = pltpu.roll(a, 1, 1)[:, start - low : start - low + size]
    if low == start or high == start + size:
        here = a[:, start - low : start - low + size]
        beyond = here if edge else jnp.zeros_like(here)
        column = lax.broadcasted_iota(jnp.int32, here.shape, 1)
        if high == start + size:
            after = jnp.where(column == size - 1, beyond, after)
        if low == start:
            before = jnp.where(column == 0, beyond, before)
    return after - before


def row_difference(a, above, below):
    rows = a.shape[0]
    row = lax.broadcasted_iota(jnp.int32, a.shape, 0)
    after = jnp.where(row == rows - 1, below, pltpu.roll(a, rows - 1, 0))
    before = jnp.where(row == 0, above, pltpu.roll(a, 1, 0))
    return after - before


def exchange(axis, number, source, target, device, send_sem, recv_sem):
    return pltpu.make_async_remote_copy(
        src_ref=source, dst_ref=target, send_sem=send_sem.at[number], recv_sem=recv_sem.at[number],
        device_id={axis: device}, device_id_type=MESH,
    )


def advance_kernel(
    count, groups,
    fields, depth, coriolis, drag, rim, out,
    flux_c, keep_c, turn_c, push_c, rim_c, send, recv, last_send, last_recv, halo, near, far,
    send_sem, recv_sem,
):
    members, _, rows, width = out.shape
    each = members // groups
    me = lax.axis_index("space")
    towards = (lax.rem(me + count - 1, count), lax.rem(me + 1, count))

    barrier = pltpu.get_barrier_semaphore()
    for neighbour in towards:
        pl.semaphore_signal(barrier, inc=1, device_id={"space": neighbour}, device_id_type=MESH)

    def swap(step, group, side):
        number = 2 * (step * groups + group) + side
        if step == STEPS:
            source, target = last_send.at[group, side], last_recv.at[group, 1 - side]
        else:
            source, target = send.at[step, group, side], recv.at[step, group, 1 - side]
        return exchange("space", number, source, target, towards[side], send_sem, recv_sem)

    for group in range(groups):
        for side, row in ((UP, 0), (DOWN, rows - 1)):
            for i in range(each):
                for k in range(2):
                    at = slice(k * each + i, k * each + i + 1)
                    send[0, group, side, at, :] = fields[group * each + i, 1 + k, row : row + 1, :]
    pl.semaphore_wait(barrier, 2)
    for group in range(groups):
        for side in (UP, DOWN):
            swap(0, group, side).start()

    keep = 1.0 / (1.0 + DT * drag[...])
    flux_c[...] = 0.5 * DT * depth[...]
    keep_c[...] = keep
    turn_c[...] = DT * coriolis[...] * keep
    push_c[...] = 0.5 * DT * keep
    for side in (UP, DOWN):
        rim_depth, rim_coriolis, rim_drag = (rim[side, k : k + 1, :] for k in range(3))
        k = 1.0 / (1.0 + DT * rim_drag)
        for i in range(each):
            at = slice(side * each + i, side * each + i + 1)
            rim_c[0, at, :] = 0.5 * DT * rim_depth
            rim_c[1, at, :] = k
            rim_c[2, at, :] = DT * rim_coriolis * k
            rim_c[3, at, :] = 0.5 * DT * k
            rim_c[4, at, :] = 0.5 * DT * k if side == UP else -0.5 * DT * k

    chunk = min(512, width)
    chunks = [(start, pl.ds(start, chunk)) for start in range(0, width, chunk)]

    def arrived(step, group):
        for side in (UP, DOWN):
            swap(step, group, side).wait_recv()
        return last_recv.at[group] if step == STEPS else recv.at[step, group]

    def beside(step, group, come):
        for side in (UP, DOWN):
            at = slice(side * each, (side + 1) * each)
            near[at, :] = come[side, 0:each, :]
            far[at, :] = send[step, group, side, 0:each, :] - come[side, each : 2 * each, :]
        u, v = halo[group, 0], halo[group, 1]
        slope = column_difference(lambda low, high: near[:, low:high], 0, width, width, True)
        halo[group, 0] = u * rim_c[1] + v * rim_c[2] - rim_c[3] * slope
        halo[group, 1] = v * rim_c[1] - u * rim_c[2] - rim_c[4] * far[...]

    def along(p, i, come, at):
        return out[p, 2, :, at] - push_c[:, at] * row_difference(
            out[p, 0, :, at], come[UP, i : i + 1, at], come[DOWN, i : i + 1, at]
        )

    for step in range(1, STEPS + 1):
        old = fields if step == 1 else out
        for group in range(groups):
            come = arrived(step - 1, group)
            if step == 1:
                for side in (UP, DOWN):
                    for k in range(2):
                        halo[group, k, side * each : (side + 1) * each, :] = come[
                            side, k * each : (k + 1) * each, :
                        ]
            else:
                beside(step - 1, group, come)
            near[...] = rim_c[0] * halo[group, 1]
            for i in range(each):
                p = group * each + i
                for start, at in chunks:
                    if step == 1:
                        v = fields[p, 2, :, at]
                    else:
                        v = along(p, i, come, at)
                        out[p, 2, :, at] = v
                    outflow = column_difference(
                        lambda low, high: flux_c[:, low:high] * old[p, 1, :, low:high], start, chunk, width, False
                    )
                    height = old[p, 0, :, at] - (
                        outflow
                        + row_difference(flux_c[:, at] * v, near[i : i + 1, at], near[each + i : each + i + 1, at])
                    )
                    out[p, 0, :, at] = height
                    if step == STEPS:
                        last_send[group, UP, i : i + 1, at] = height[0:1, :]
                        last_send[group, DOWN, i : i + 1, at] = height[rows - 1 : rows, :]
                    else:
                        for k in range(2):
                            n = k * each + i
                            send[step, group, UP, n : n + 1, at] = height[k : k + 1, :]
                            send[step, group, DOWN, n : n + 1, at] = height[rows - 1 - k : rows - k, :]
            for side in (UP, DOWN):
                swap(step, group, side).start()
            for i in range(each):
                p = group * each + i
                for start, at in chunks:
                    u, v = old[p, 1, :, at], (old if step == 1 else out)[p, 2, :, at]
                    slope = column_difference(
                        lambda low, high: out[p, 0, :, low:high], start, chunk, width, True
                    )
                    out[p, 1, :, at] = u * keep_c[:, at] + turn_c[:, at] * v - push_c[:, at] * slope
                    out[p, 2, :, at] = v * keep_c[:, at] - turn_c[:, at] * u
    for group in range(groups):
        come = arrived(STEPS, group)
        for i in range(each):
            p = group * each + i
            for start, at in chunks:
                out[p, 2, :, at] = along(p, i, come, at)
    for step in range(STEPS + 1):
        for group in range(groups):
            for side in (UP, DOWN):
                swap(step, group, side).wait_send()


def advance(fields, depth, coriolis, drag, rim, count):
    members, _, rows, width = fields.shape
    groups = 2
    each = members // groups
    f32 = jnp.float32
    plane = pltpu.VMEM((rows, width), f32)
    edges = pltpu.VMEM((2 * each, width), f32)
    copies = 2 * (STEPS + 1) * groups
    return pl.pallas_call(
        functools.partial(advance_kernel, count, groups),
        out_shape=jax.ShapeDtypeStruct(fields.shape, f32),
        in_specs=[pl.BlockSpec(memory_space=pltpu.VMEM)] * 5,
        out_specs=pl.BlockSpec(memory_space=pltpu.VMEM),
        scratch_shapes=[
            plane, plane, plane, plane,
            pltpu.VMEM((5, 2 * each, width), f32),
            pltpu.VMEM((STEPS, groups, 2, 2 * each, width), f32),
            pltpu.VMEM((STEPS, groups, 2, 2 * each, width), f32),
            pltpu.VMEM((groups, 2, each, width), f32),
            pltpu.VMEM((groups, 2, each, width), f32),
            pltpu.VMEM((groups, 2, 2 * each, width), f32),
            edges, edges,
            pltpu.SemaphoreType.DMA((copies,)),
            pltpu.SemaphoreType.DMA((copies,)),
        ],
        compiler_params=pltpu.CompilerParams(
            collective_id=0, has_side_effects=True, vmem_limit_bytes=40 * 1024 * 1024
        ),
        name="advance",
    )(fields, depth, coriolis, drag, rim)


def routes_kernel(members, across, out, tier_out):
    part = across.shape[1]
    me = lax.axis_index("dom")
    chip = me // 2
    lane = lax.broadcasted_iota(jnp.int32, (part, part), 1)
    sub = lax.broadcasted_iota(jnp.int32, (part, part), 0)
    row_p, col_p = lane[0:1, :], sub[:, 0:1]
    down = jnp.sum(jnp.where(lane == sub, across[...], 0), axis=1, keepdims=True)

    def over(mask, value, axis):
        return jnp.sum(jnp.where(mask, value, 0), axis=axis, keepdims=True)

    target_row = over((down == lane) & (sub != lane), sub + 1, 0) - 1
    target_col = over((across[...] == sub) & (sub != lane), lane + 1, 1) - 1

    def chip_of(p):
        return lax.shift_right_arithmetic(p, (2 * members).bit_length() - 1)

    def block_of(p):
        return lax.shift_right_arithmetic(p, members.bit_length() - 1)

    d_row = jnp.where(target_row >= 0, chip_of(row_p) ^ chip_of(target_row), 0)
    d_col = jnp.where(target_col >= 0, chip_of(col_p) ^ chip_of(target_col), 0)
    rank = over((target_col >= 0) & (sub < lane) & (block_of(sub) == block_of(lane)), 1, 0)
    own = (block_of(row_p) & 1) * CAP + rank

    columns = [None] * 8
    most_first, most_second = jnp.int32(0), jnp.int32(0)
    for q in range(2):
        first, second = 1 + q, 2 - q
        f_row, f_col = (d_row & first) != 0, (d_col & first) != 0
        g_row, g_col = (d_row & second) != 0, (d_col & second) != 0
        s1 = over(f_col & (chip_of(sub) == chip_of(lane)) & (sub < lane), 1, 0)
        e_row = chip_of(row_p) ^ (d_row & first)
        e_col = chip_of(col_p) ^ (d_col & first)
        key_row = row_p + jnp.where(f_row, part, 0)
        key_col = col_p + jnp.where(f_col, part, 0)
        s2 = over(g_col & (e_col == e_row) & (key_col < key_row), 1, 0)
        found = jnp.where(g_row, 4 * CAP + s2, jnp.where(f_row, 2 * CAP + s1, own))
        columns[q] = over((s1 == sub) & f_row & (chip_of(row_p) == chip), own, 1)
        columns[2 + q] = over(
            (s2 == sub) & g_row & (e_row == chip), jnp.where(f_row, 2 * CAP + s1, own), 1
        )
        columns[4 + q] = over(target_row == sub, found, 1)
        most_first = jnp.maximum(most_first, jnp.max(jnp.where(f_row, s1 + 1, 0)))
        most_second = jnp.maximum(most_second, jnp.max(jnp.where(g_row, s2 + 1, 0)))
    columns[6] = jnp.where(down != col_p, 1, 0)
    tier = jnp.int32(len(TIERS))
    for n in range(len(TIERS) - 1, -1, -1):
        fits = (most_first <= TIERS[n][0]) & (most_second <= TIERS[n][1])
        tier = jnp.where(fits, n, tier)
    mine = over((rank == sub) & (target_row >= 0) & (block_of(row_p) == me), row_p & (members - 1), 1)
    columns[7] = mine
    tier_out[0] = tier
    for k in range(8):
        out[:, k : k + 1] = columns[k]


TIERS = ((2, 2), (3, 3), (4, 4))
PIECES = 4


def resample_kernel(
    c1, c2, count,
    table, state, jitter, depth, coriolis, drag, out, rim,
    rim_send, core_send, last_send, last_recv, own_all, first_send_all, first_recv_all, second_send_all, second_recv_all,
    send_sem, recv_sem, rim_send_sem, rim_recv_sem,
):
    members, _, rows, width = out.shape
    half, wide = rows // 2, width // PIECES
    pieces = range(PIECES)
    me = lax.axis_index("dom")
    core = lax.rem(me, 2)
    chip = me // 2
    other = me + 1 - 2 * core
    turned = (me + 2 - 4 * lax.rem(chip, 2), me + 4 - 8 * (chip // 2))
    slab = lax.axis_index("space")
    towards = (lax.rem(slab + count - 1, count), lax.rem(slab + 1, count))
    mine, theirs = pl.multiple_of(core * half, half), pl.multiple_of((1 - core) * half, half)

    barrier = pltpu.get_barrier_semaphore()
    for device in (other,) + turned:
        pl.semaphore_signal(barrier, inc=1, device_id={"dom": device}, device_id_type=MESH)
    for neighbour in towards:
        pl.semaphore_signal(barrier, inc=1, device_id={"space": neighbour}, device_id_type=MESH)

    def send(number, source, target, device):
        return exchange("dom", number, source, target, device, send_sem, recv_sem)

    rims = [
        exchange("space", side, rim_send.at[side], rim.at[1 - side], towards[side], rim_send_sem, rim_recv_sem)
        for side in (UP, DOWN)
    ]
    own, first_send, first_recv, second_send, second_recv = (
        tuple(ref for ref in refs) for refs in
        (own_all, first_send_all, first_recv_all, second_send_all, second_recv_all)
    )
    cores = [send(t, core_send.at[t], own[t].at[pl.ds(core * CAP, CAP)], other) for t in pieces]
    firsts = [send(PIECES + t, first_send[t], first_recv[t], turned[t % 2]) for t in pieces]
    seconds = [send(2 * PIECES + t, second_send[t], second_recv[t], turned[1 - t % 2]) for t in pieces]
    lasts = [send(3 * PIECES + t, last_send.at[t], last_recv.at[t], other) for t in pieces]

    for side, row in ((UP, 0), (DOWN, rows - 1)):
        for k, plane in enumerate((depth, coriolis, drag, drag)):
            rim_send[side, k : k + 1, :] = plane[row : row + 1, :]
    for t in pieces:
        columns = pl.ds(t * wide, wide)
        for k in range(CAP):
            slot = table[k, 7]
            core_send[t, k] = state[slot, :, pl.ds(theirs, half), columns]
            own[t][core * CAP + k] = state[slot, :, pl.ds(mine, half), columns]
    pl.semaphore_wait(barrier, 5)
    for t in pieces:
        cores[t].start()
    for copy in rims:
        copy.start()
    for t in pieces:
        cores[t].wait_recv()
        for k in range(c1):
            first_send[t][k] = own[t][table[k, t % 2]]
        firsts[t].start()

    def pick(t, index, come):
        value = own[t][jnp.clip(index, 0, 2 * CAP - 1)]
        value = jnp.where(index >= 2 * CAP, first_recv[t][jnp.clip(index - 2 * CAP, 0, c1 - 1)], value)
        if come:
            value = jnp.where(
                index >= 4 * CAP, second_recv[t][jnp.clip(index - 4 * CAP, 0, c2 - 1)], value
            )
        return value

    for t in pieces:
        firsts[t].wait_recv()
        for k in range(c2):
            second_send[t][k] = pick(t, table[k, 2 + t % 2], False)
        seconds[t].start()
    for t in pieces:
        seconds[t].wait_recv()
        for k in range(members):
            last_send[t, k] = pick(t, table[other * members + k, 4 + t % 2], True)
        lasts[t].start()
        columns = pl.ds(t * wide, wide)
        for k in range(members):
            got = pick(t, table[me * members + k, 4 + t % 2], True)
            kept = state[k, :, pl.ds(mine, half), columns]
            out[k, :, pl.ds(mine, half), columns] = (
                jnp.where(table[me * members + k, 6] != 0, got, kept) + jitter[k, :, pl.ds(mine, half), columns]
            )
    for t in pieces:
        lasts[t].wait_recv()
        columns = pl.ds(t * wide, wide)
        for k in range(members):
            kept = state[k, :, pl.ds(theirs, half), columns]
            out[k, :, pl.ds(theirs, half), columns] = (
                jnp.where(table[me * members + k, 6] != 0, last_recv[t, k], kept)
                + jitter[k, :, pl.ds(theirs, half), columns]
            )
    for copy in rims:
        copy.wait()
    for copy in cores + firsts + seconds + lasts:
        copy.wait_send()


def resample(number, c1, c2, count, table, state, jitter, depth, coriolis, drag):
    members, parts, rows, width = state.shape
    f32 = jnp.float32
    vmem = pl.BlockSpec(memory_space=pltpu.VMEM)

    def slots(*lead):
        return pltpu.VMEM((*lead, parts, rows // 2, width // PIECES), f32)

    return pl.pallas_call(
        functools.partial(resample_kernel, c1, c2, count),
        out_shape=(
            jax.ShapeDtypeStruct(state.shape, f32), jax.ShapeDtypeStruct((2, 4, width), f32),
        ),
        in_specs=[pl.BlockSpec(memory_space=pltpu.SMEM)] + [vmem] * 5,
        out_specs=(vmem, vmem),
        scratch_shapes=[
            pltpu.VMEM((2, 4, width), f32),
            slots(PIECES, CAP), slots(PIECES, members), slots(PIECES, members),
            [slots(2 * CAP)] * PIECES, [slots(c1)] * PIECES, [slots(c1)] * PIECES,
            [slots(c2)] * PIECES, [slots(c2)] * PIECES,
            pltpu.SemaphoreType.DMA((4 * PIECES,)), pltpu.SemaphoreType.DMA((4 * PIECES,)),
            pltpu.SemaphoreType.DMA((2,)), pltpu.SemaphoreType.DMA((2,)),
        ],
        compiler_params=pltpu.CompilerParams(
            collective_id=number, has_side_effects=True, vmem_limit_bytes=40 * 1024 * 1024
        ),
        name="resample",
    )(table, state, jitter, depth, coriolis, drag)


def routed(count, ancestor, state, jitter, *planes):
    members = state.shape[0]
    part = ancestor.shape[0]
    table, tier = pl.pallas_call(
        functools.partial(routes_kernel, members),
        out_shape=(
            jax.ShapeDtypeStruct((part, 8), jnp.int32), jax.ShapeDtypeStruct((1,), jnp.int32),
        ),
        in_specs=[pl.BlockSpec(memory_space=pltpu.VMEM)],
        out_specs=(pl.BlockSpec(memory_space=pltpu.VMEM), pl.BlockSpec(memory_space=pltpu.SMEM)),
        name="routes",
    )(ancestor[None, :])
    sizes = TIERS + ((2 * CAP, 2 * members),)
    return lax.switch(
        tier[0],
        [functools.partial(resample, 1 + n, c1, c2, count) for n, (c1, c2) in enumerate(sizes)],
        table, state, jitter, *planes,
    )


def edge_rows(count, *planes):
    stacked = jnp.stack(planes + planes[-1:])
    after = [(i, (i + 1) % count) for i in range(count)]
    before = [((i + 1) % count, i) for i in range(count)]
    return jnp.stack(
        [lax.ppermute(stacked[:, -1], "space", after), lax.ppermute(stacked[:, 0], "space", before)]
    )


def gathered(ancestor, state, jitter):
    members = state.shape[0]
    part = ancestor.shape[0]
    first = lax.axis_index("dom") * members
    index = jnp.arange(part, dtype=jnp.int32)
    moved = ancestor != index
    donor = jnp.any((ancestor[:, None] == index[None, :]) & moved[:, None], axis=0)
    earlier = (index[None, :] < index[:, None]) & (index[None, :] // members == index[:, None] // members)
    place = jnp.sum((earlier & donor[None, :]).astype(jnp.int32), axis=1)
    sent = []
    for k in range(CAP):
        hit = donor & (place == k) & (index // members == first // members)
        slot = jnp.sum(jnp.where(hit, index - first, 0))
        sent.append(lax.dynamic_slice_in_dim(state, slot, 1))
    pool = lax.all_gather(jnp.concatenate(sent), "dom", axis=0, tiled=True)
    where = (ancestor // members) * CAP + jnp.sum(
        jnp.where(ancestor[:, None] == index[None, :], place[None, :], 0), axis=1
    )
    copied = []
    for k in range(members):
        j = first + k
        got = lax.dynamic_slice_in_dim(pool, where[j], 1)
        copied.append(jnp.where(moved[j], got, state[k : k + 1]))
    return jnp.concatenate(copied) + jitter


def local(count, doms, ancestor, state, jitter, depth, coriolis, drag):
    members = state.shape[0]
    simple = doms == 8 and members == 4 and state.shape[2] % 16 == 0
    planes = (depth, coriolis, drag)
    if simple:
        fields, rim = routed(count, ancestor, state, jitter, *planes)
    else:
        fields, rim = gathered(ancestor, state, jitter), edge_rows(count, *planes)
    return advance(fields, *planes, rim, count)


def solution(mesh):
    field = P("dom", None, "space", None)
    plane = P("space", None)
    return jax.shard_map(
        functools.partial(local, mesh.shape["space"], mesh.shape["dom"]),
        mesh=mesh,
        in_specs=(P(), field, field, plane, plane, plane),
        out_specs=field,
        check_vma=False,
    )
```

```python
import functools

import jax
import jax.numpy as jnp
from jax import lax
from jax.experimental import pallas as pl
from jax.experimental.pallas import tpu as pltpu
from jax.sharding import PartitionSpec as P

STEPS = 4
DT = 0.3
CAP = 2
MESH = pl.DeviceIdType.MESH
UP, DOWN = 0, 1


def column_difference(load, start, size, width, edge):
    low, high = max(start - 128, 0), min(start + size + 128, width)
    a = load(low, high)
    after = pltpu.roll(a, high - low - 1, 1)[:, start - low : start - low + size]
    before = pltpu.roll(a, 1, 1)[:, start - low : start - low + size]
    if low == start or high == start + size:
        here = a[:, start - low : start - low + size]
        beyond = here if edge else jnp.zeros_like(here)
        column = lax.broadcasted_iota(jnp.int32, here.shape, 1)
        if high == start + size:
            after = jnp.where(column == size - 1, beyond, after)
        if low == start:
            before = jnp.where(column == 0, beyond, before)
    return after - before


def row_difference(a, above, below):
    rows = a.shape[0]
    row = lax.broadcasted_iota(jnp.int32, a.shape, 0)
    after = jnp.where(row == rows - 1, below, pltpu.roll(a, rows - 1, 0))
    before = jnp.where(row == 0, above, pltpu.roll(a, 1, 0))
    return after - before


def exchange(axis, number, source, target, device, send_sem, recv_sem):
    return pltpu.make_async_remote_copy(
        src_ref=source, dst_ref=target, send_sem=send_sem.at[number], recv_sem=recv_sem.at[number],
        device_id={axis: device}, device_id_type=MESH,
    )


def advance_kernel(
    count, groups,
    fields, depth, coriolis, drag, rim, out,
    flux_c, keep_c, turn_c, push_c, rim_c, send, recv, last_send, last_recv, halo, near, far,
    send_sem, recv_sem,
):
    members, _, rows, width = out.shape
    each = members // groups
    me = lax.axis_index("space")
    towards = (lax.rem(me + count - 1, count), lax.rem(me + 1, count))

    barrier = pltpu.get_barrier_semaphore()
    for neighbour in towards:
        pl.semaphore_signal(barrier, inc=1, device_id={"space": neighbour}, device_id_type=MESH)

    def swap(step, group, side):
        number = 2 * (step * groups + group) + side
        if step == STEPS:
            source, target = last_send.at[group, side], last_recv.at[group, 1 - side]
        else:
            source, target = send.at[step, group, side], recv.at[step, group, 1 - side]
        return exchange("space", number, source, target, towards[side], send_sem, recv_sem)

    for group in range(groups):
        for side, row in ((UP, 0), (DOWN, rows - 1)):
            for i in range(each):
                for k in range(2):
                    at = slice(k * each + i, k * each + i + 1)
                    send[0, group, side, at, :] = fields[group * each + i, 1 + k, row : row + 1, :]
    pl.semaphore_wait(barrier, 2)
    for group in range(groups):
        for side in (UP, DOWN):
            swap(0, group, side).start()

    keep = 1.0 / (1.0 + DT * drag[...])
    flux_c[...] = 0.5 * DT * depth[...]
    keep_c[...] = keep
    turn_c[...] = DT * coriolis[...] * keep
    push_c[...] = 0.5 * DT * keep
    for side in (UP, DOWN):
        rim_depth, rim_coriolis, rim_drag = (rim[side, k : k + 1, :] for k in range(3))
        k = 1.0 / (1.0 + DT * rim_drag)
        for i in range(each):
            at = slice(side * each + i, side * each + i + 1)
            rim_c[0, at, :] = 0.5 * DT * rim_depth
            rim_c[1, at, :] = k
            rim_c[2, at, :] = DT * rim_coriolis * k
            rim_c[3, at, :] = 0.5 * DT * k
            rim_c[4, at, :] = 0.5 * DT * k if side == UP else -0.5 * DT * k

    chunk = min(512, width)
    chunks = [(start, pl.ds(start, chunk)) for start in range(0, width, chunk)]

    def arrived(step, group):
        for side in (UP, DOWN):
            swap(step, group, side).wait_recv()
        return last_recv.at[group] if step == STEPS else recv.at[step, group]

    def beside(step, group, come):
        for side in (UP, DOWN):
            at = slice(side * each, (side + 1) * each)
            near[at, :] = come[side, 0:each, :]
            far[at, :] = send[step, group, side, 0:each, :] - come[side, each : 2 * each, :]
        u, v = halo[group, 0], halo[group, 1]
        slope = column_difference(lambda low, high: near[:, low:high], 0, width, width, True)
        halo[group, 0] = u * rim_c[1] + v * rim_c[2] - rim_c[3] * slope
        halo[group, 1] = v * rim_c[1] - u * rim_c[2] - rim_c[4] * far[...]

    def along(p, i, come, at):
        return out[p, 2, :, at] - push_c[:, at] * row_difference(
            out[p, 0, :, at], come[UP, i : i + 1, at], come[DOWN, i : i + 1, at]
        )

    for step in range(1, STEPS + 1):
        old = fields if step == 1 else out
        for group in range(groups):
            come = arrived(step - 1, group)
            if step == 1:
                for side in (UP, DOWN):
                    for k in range(2):
                        halo[group, k, side * each : (side + 1) * each, :] = come[
                            side, k * each : (k + 1) * each, :
                        ]
            else:
                beside(step - 1, group, come)
            near[...] = rim_c[0] * halo[group, 1]
            for i in range(each):
                p = group * each + i
                for start, at in chunks:
                    if step == 1:
                        v = fields[p, 2, :, at]
                    else:
                        v = along(p, i, come, at)
                        out[p, 2, :, at] = v
                    outflow = column_difference(
                        lambda low, high: flux_c[:, low:high] * old[p, 1, :, low:high], start, chunk, width, False
                    )
                    height = old[p, 0, :, at] - (
                        outflow
                        + row_difference(flux_c[:, at] * v, near[i : i + 1, at], near[each + i : each + i + 1, at])
                    )
                    out[p, 0, :, at] = height
                    if step == STEPS:
                        last_send[group, UP, i : i + 1, at] = height[0:1, :]
                        last_send[group, DOWN, i : i + 1, at] = height[rows - 1 : rows, :]
                    else:
                        for k in range(2):
                            n = k * each + i
                            send[step, group, UP, n : n + 1, at] = height[k : k + 1, :]
                            send[step, group, DOWN, n : n + 1, at] = height[rows - 1 - k : rows - k, :]
            for side in (UP, DOWN):
                swap(step, group, side).start()
            for i in range(each):
                p = group * each + i
                for start, at in chunks:
                    u, v = old[p, 1, :, at], (old if step == 1 else out)[p, 2, :, at]
                    slope = column_difference(
                        lambda low, high: out[p, 0, :, low:high], start, chunk, width, True
                    )
                    out[p, 1, :, at] = u * keep_c[:, at] + turn_c[:, at] * v - push_c[:, at] * slope
                    out[p, 2, :, at] = v * keep_c[:, at] - turn_c[:, at] * u
    for group in range(groups):
        come = arrived(STEPS, group)
        for i in range(each):
            p = group * each + i
            for start, at in chunks:
                out[p, 2, :, at] = along(p, i, come, at)
    for step in range(STEPS + 1):
        for group in range(groups):
            for side in (UP, DOWN):
                swap(step, group, side).wait_send()


def advance(fields, depth, coriolis, drag, rim, count):
    members, _, rows, width = fields.shape
    groups = members
    each = members // groups
    f32 = jnp.float32
    plane = pltpu.VMEM((rows, width), f32)
    edges = pltpu.VMEM((2 * each, width), f32)
    copies = 2 * (STEPS + 1) * groups
    return pl.pallas_call(
        functools.partial(advance_kernel, count, groups),
        out_shape=jax.ShapeDtypeStruct(fields.shape, f32),
        in_specs=[pl.BlockSpec(memory_space=pltpu.VMEM)] * 5,
        out_specs=pl.BlockSpec(memory_space=pltpu.VMEM),
        scratch_shapes=[
            plane, plane, plane, plane,
            pltpu.VMEM((5, 2 * each, width), f32),
            pltpu.VMEM((STEPS, groups, 2, 2 * each, width), f32),
            pltpu.VMEM((STEPS, groups, 2, 2 * each, width), f32),
            pltpu.VMEM((groups, 2, each, width), f32),
            pltpu.VMEM((groups, 2, each, width), f32),
            pltpu.VMEM((groups, 2, 2 * each, width), f32),
            edges, edges,
            pltpu.SemaphoreType.DMA((copies,)),
            pltpu.SemaphoreType.DMA((copies,)),
        ],
        compiler_params=pltpu.CompilerParams(
            collective_id=0, has_side_effects=True, vmem_limit_bytes=40 * 1024 * 1024
        ),
        name="advance",
    )(fields, depth, coriolis, drag, rim)


def routes_kernel(members, across, out, tier_out):
    part = across.shape[1]
    me = lax.axis_index("dom")
    chip = me // 2
    lane = lax.broadcasted_iota(jnp.int32, (part, part), 1)
    sub = lax.broadcasted_iota(jnp.int32, (part, part), 0)
    row_p, col_p = lane[0:1, :], sub[:, 0:1]
    down = jnp.sum(jnp.where(lane == sub, across[...], 0), axis=1, keepdims=True)

    def over(mask, value, axis):
        return jnp.sum(jnp.where(mask, value, 0), axis=axis, keepdims=True)

    target_row = over((down == lane) & (sub != lane), sub + 1, 0) - 1
    target_col = over((across[...] == sub) & (sub != lane), lane + 1, 1) - 1

    def chip_of(p):
        return lax.shift_right_arithmetic(p, (2 * members).bit_length() - 1)

    def block_of(p):
        return lax.shift_right_arithmetic(p, members.bit_length() - 1)

    d_row = jnp.where(target_row >= 0, chip_of(row_p) ^ chip_of(target_row), 0)
    d_col = jnp.where(target_col >= 0, chip_of(col_p) ^ chip_of(target_col), 0)
    rank = over((target_col >= 0) & (sub < lane) & (block_of(sub) == block_of(lane)), 1, 0)
    own = (block_of(row_p) & 1) * CAP + rank

    columns = [None] * 8
    most_first, most_second = jnp.int32(0), jnp.int32(0)
    for q in range(2):
        first, second = 1 + q, 2 - q
        f_row, f_col = (d_row & first) != 0, (d_col & first) != 0
        g_row, g_col = (d_row & second) != 0, (d_col & second) != 0
        s1 = over(f_col & (chip_of(sub) == chip_of(lane)) & (sub < lane), 1, 0)
        e_row = chip_of(row_p) ^ (d_row & first)
        e_col = chip_of(col_p) ^ (d_col & first)
        key_row = row_p + jnp.where(f_row, part, 0)
        key_col = col_p + jnp.where(f_col, part, 0)
        s2 = over(g_col & (e_col == e_row) & (key_col < key_row), 1, 0)
        found = jnp.where(g_row, 4 * CAP + s2, jnp.where(f_row, 2 * CAP + s1, own))
        columns[q] = over((s1 == sub) & f_row & (chip_of(row_p) == chip), own, 1)
        columns[2 + q] = over(
            (s2 == sub) & g_row & (e_row == chip), jnp.where(f_row, 2 * CAP + s1, own), 1
        )
        columns[4 + q] = over(target_row == sub, found, 1)
        most_first = jnp.maximum(most_first, jnp.max(jnp.where(f_row, s1 + 1, 0)))
        most_second = jnp.maximum(most_second, jnp.max(jnp.where(g_row, s2 + 1, 0)))
    columns[6] = jnp.where(down != col_p, 1, 0)
    tier = jnp.int32(len(TIERS))
    for n in range(len(TIERS) - 1, -1, -1):
        fits = (most_first <= TIERS[n][0]) & (most_second <= TIERS[n][1])
        tier = jnp.where(fits, n, tier)
    mine = over((rank == sub) & (target_row >= 0) & (block_of(row_p) == me), row_p & (members - 1), 1)
    columns[7] = mine
    tier_out[0] = tier
    for k in range(8):
        out[:, k : k + 1] = columns[k]


TIERS = ((2, 2), (3, 3), (4, 4))
PIECES = 4


def resample_kernel(
    c1, c2, count,
    table, state, jitter, depth, coriolis, drag, out, rim,
    rim_send, core_send, last_send, last_recv, own_all, first_send_all, first_recv_all, second_send_all, second_recv_all,
    send_sem, recv_sem, rim_send_sem, rim_recv_sem,
):
    members, _, rows, width = out.shape
    half, wide = rows // 2, width // PIECES
    pieces = range(PIECES)
    me = lax.axis_index("dom")
    core = lax.rem(me, 2)
    chip = me // 2
    other = me + 1 - 2 * core
    turned = (me + 2 - 4 * lax.rem(chip, 2), me + 4 - 8 * (chip // 2))
    slab = lax.axis_index("space")
    towards = (lax.rem(slab + count - 1, count), lax.rem(slab + 1, count))
    mine, theirs = pl.multiple_of(core * half, half), pl.multiple_of((1 - core) * half, half)

    barrier = pltpu.get_barrier_semaphore()
    for device in (other,) + turned:
        pl.semaphore_signal(barrier, inc=1, device_id={"dom": device}, device_id_type=MESH)
    for neighbour in towards:
        pl.semaphore_signal(barrier, inc=1, device_id={"space": neighbour}, device_id_type=MESH)

    def send(number, source, target, device):
        return exchange("dom", number, source, target, device, send_sem, recv_sem)

    rims = [
        exchange("space", side, rim_send.at[side], rim.at[1 - side], towards[side], rim_send_sem, rim_recv_sem)
        for side in (UP, DOWN)
    ]
    own, first_send, first_recv, second_send, second_recv = (
        tuple(ref for ref in refs) for refs in
        (own_all, first_send_all, first_recv_all, second_send_all, second_recv_all)
    )
    cores = [send(t, core_send.at[t], own[t].at[pl.ds(core * CAP, CAP)], other) for t in pieces]
    firsts = [send(PIECES + t, first_send[t], first_recv[t], turned[t % 2]) for t in pieces]
    seconds = [send(2 * PIECES + t, second_send[t], second_recv[t], turned[1 - t % 2]) for t in pieces]
    lasts = [send(3 * PIECES + t, last_send.at[t], last_recv.at[t], other) for t in pieces]

    for side, row in ((UP, 0), (DOWN, rows - 1)):
        for k, plane in enumerate((depth, coriolis, drag, drag)):
            rim_send[side, k : k + 1, :] = plane[row : row + 1, :]
    for t in pieces:
        columns = pl.ds(t * wide, wide)
        for k in range(CAP):
            slot = table[k, 7]
            core_send[t, k] = state[slot, :, pl.ds(theirs, half), columns]
            own[t][core * CAP + k] = state[slot, :, pl.ds(mine, half), columns]
    pl.semaphore_wait(barrier, 5)
    for t in pieces:
        cores[t].start()
    for copy in rims:
        copy.start()
    for t in pieces:
        cores[t].wait_recv()
        for k in range(c1):
            first_send[t][k] = own[t][table[k, t % 2]]
        firsts[t].start()

    def pick(t, index, come):
        value = own[t][jnp.clip(index, 0, 2 * CAP - 1)]
        value = jnp.where(index >= 2 * CAP, first_recv[t][jnp.clip(index - 2 * CAP, 0, c1 - 1)], value)
        if come:
            value = jnp.where(
                index >= 4 * CAP, second_recv[t][jnp.clip(index - 4 * CAP, 0, c2 - 1)], value
            )
        return value

    for t in pieces:
        firsts[t].wait_recv()
        for k in range(c2):
            second_send[t][k] = pick(t, table[k, 2 + t % 2], False)
        seconds[t].start()
    for t in pieces:
        seconds[t].wait_recv()
        for k in range(members):
            last_send[t, k] = pick(t, table[other * members + k, 4 + t % 2], True)
        lasts[t].start()
        columns = pl.ds(t * wide, wide)
        for k in range(members):
            got = pick(t, table[me * members + k, 4 + t % 2], True)
            kept = state[k, :, pl.ds(mine, half), columns]
            out[k, :, pl.ds(mine, half), columns] = (
                jnp.where(table[me * members + k, 6] != 0, got, kept) + jitter[k, :, pl.ds(mine, half), columns]
            )
    for t in pieces:
        lasts[t].wait_recv()
        columns = pl.ds(t * wide, wide)
        for k in range(members):
            kept = state[k, :, pl.ds(theirs, half), columns]
            out[k, :, pl.ds(theirs, half), columns] = (
                jnp.where(table[me * members + k, 6] != 0, last_recv[t, k], kept)
                + jitter[k, :, pl.ds(theirs, half), columns]
            )
    for copy in rims:
        copy.wait()
    for copy in cores + firsts + seconds + lasts:
        copy.wait_send()


def resample(number, c1, c2, count, table, state, jitter, depth, coriolis, drag):
    members, parts, rows, width = state.shape
    f32 = jnp.float32
    vmem = pl.BlockSpec(memory_space=pltpu.VMEM)

    def slots(*lead):
        return pltpu.VMEM((*lead, parts, rows // 2, width // PIECES), f32)

    return pl.pallas_call(
        functools.partial(resample_kernel, c1, c2, count),
        out_shape=(
            jax.ShapeDtypeStruct(state.shape, f32), jax.ShapeDtypeStruct((2, 4, width), f32),
        ),
        in_specs=[pl.BlockSpec(memory_space=pltpu.SMEM)] + [vmem] * 5,
        out_specs=(vmem, vmem),
        scratch_shapes=[
            pltpu.VMEM((2, 4, width), f32),
            slots(PIECES, CAP), slots(PIECES, members), slots(PIECES, members),
            [slots(2 * CAP)] * PIECES, [slots(c1)] * PIECES, [slots(c1)] * PIECES,
            [slots(c2)] * PIECES, [slots(c2)] * PIECES,
            pltpu.SemaphoreType.DMA((4 * PIECES,)), pltpu.SemaphoreType.DMA((4 * PIECES,)),
            pltpu.SemaphoreType.DMA((2,)), pltpu.SemaphoreType.DMA((2,)),
        ],
        compiler_params=pltpu.CompilerParams(
            collective_id=number, has_side_effects=True, vmem_limit_bytes=40 * 1024 * 1024
        ),
        name="resample",
    )(table, state, jitter, depth, coriolis, drag)


def routed(count, ancestor, state, jitter, *planes):
    members = state.shape[0]
    part = ancestor.shape[0]
    table, tier = pl.pallas_call(
        functools.partial(routes_kernel, members),
        out_shape=(
            jax.ShapeDtypeStruct((part, 8), jnp.int32), jax.ShapeDtypeStruct((1,), jnp.int32),
        ),
        in_specs=[pl.BlockSpec(memory_space=pltpu.VMEM)],
        out_specs=(pl.BlockSpec(memory_space=pltpu.VMEM), pl.BlockSpec(memory_space=pltpu.SMEM)),
        name="routes",
    )(ancestor[None, :])
    sizes = TIERS + ((2 * CAP, 2 * members),)
    return lax.switch(
        tier[0],
        [functools.partial(resample, 1 + n, c1, c2, count) for n, (c1, c2) in enumerate(sizes)],
        table, state, jitter, *planes,
    )


def edge_rows(count, *planes):
    stacked = jnp.stack(planes + planes[-1:])
    after = [(i, (i + 1) % count) for i in range(count)]
    before = [((i + 1) % count, i) for i in range(count)]
    return jnp.stack(
        [lax.ppermute(stacked[:, -1], "space", after), lax.ppermute(stacked[:, 0], "space", before)]
    )


def gathered(ancestor, state, jitter):
    members = state.shape[0]
    part = ancestor.shape[0]
    first = lax.axis_index("dom") * members
    index = jnp.arange(part, dtype=jnp.int32)
    moved = ancestor != index
    donor = jnp.any((ancestor[:, None] == index[None, :]) & moved[:, None], axis=0)
    earlier = (index[None, :] < index[:, None]) & (index[None, :] // members == index[:, None] // members)
    place = jnp.sum((earlier & donor[None, :]).astype(jnp.int32), axis=1)
    sent = []
    for k in range(CAP):
        hit = donor & (place == k) & (index // members == first // members)
        slot = jnp.sum(jnp.where(hit, index - first, 0))
        sent.append(lax.dynamic_slice_in_dim(state, slot, 1))
    pool = lax.all_gather(jnp.concatenate(sent), "dom", axis=0, tiled=True)
    where = (ancestor // members) * CAP + jnp.sum(
        jnp.where(ancestor[:, None] == index[None, :], place[None, :], 0), axis=1
    )
    copied = []
    for k in range(members):
        j = first + k
        got = lax.dynamic_slice_in_dim(pool, where[j], 1)
        copied.append(jnp.where(moved[j], got, state[k : k + 1]))
    return jnp.concatenate(copied) + jitter


def local(count, doms, ancestor, state, jitter, depth, coriolis, drag):
    members = state.shape[0]
    simple = doms == 8 and members == 4 and state.shape[2] % 16 == 0
    planes = (depth, coriolis, drag)
    if simple:
        fields, rim = routed(count, ancestor, state, jitter, *planes)
    else:
        fields, rim = gathered(ancestor, state, jitter), edge_rows(count, *planes)
    return advance(fields, *planes, rim, count)


def solution(mesh):
    field = P("dom", None, "space", None)
    plane = P("space", None)
    return jax.shard_map(
        functools.partial(local, mesh.shape["space"], mesh.shape["dom"]),
        mesh=mesh,
        in_specs=(P(), field, field, plane, plane, plane),
        out_specs=field,
        check_vma=False,
    )
```

```python
import functools

import jax
import jax.numpy as jnp
from jax import lax
from jax.experimental import pallas as pl
from jax.experimental.pallas import tpu as pltpu
from jax.sharding import PartitionSpec as P

STEPS = 4
DT = 0.3
CAP = 2
MESH = pl.DeviceIdType.MESH
UP, DOWN = 0, 1


def column_difference(load, start, size, width, edge):
    low, high = max(start - 128, 0), min(start + size + 128, width)
    a = load(low, high)
    after = pltpu.roll(a, high - low - 1, 1)[:, start - low : start - low + size]
    before = pltpu.roll(a, 1, 1)[:, start - low : start - low + size]
    if low == start or high == start + size:
        here = a[:, start - low : start - low + size]
        beyond = here if edge else jnp.zeros_like(here)
        column = lax.broadcasted_iota(jnp.int32, here.shape, 1)
        if high == start + size:
            after = jnp.where(column == size - 1, beyond, after)
        if low == start:
            before = jnp.where(column == 0, beyond, before)
    return after - before


def row_difference(a, above, below):
    rows = a.shape[0]
    row = lax.broadcasted_iota(jnp.int32, a.shape, 0)
    after = jnp.where(row == rows - 1, below, pltpu.roll(a, rows - 1, 0))
    before = jnp.where(row == 0, above, pltpu.roll(a, 1, 0))
    return after - before


def exchange(axis, number, source, target, device, send_sem, recv_sem):
    return pltpu.make_async_remote_copy(
        src_ref=source, dst_ref=target, send_sem=send_sem.at[number], recv_sem=recv_sem.at[number],
        device_id={axis: device}, device_id_type=MESH,
    )


def advance_kernel(
    count, groups, greet,
    fields, depth, coriolis, drag, rim, out,
    flux_c, keep_c, turn_c, push_c, rim_c, send, recv, last_send, last_recv, halo, near, far,
    send_sem, recv_sem,
):
    members, _, rows, width = out.shape
    each = members // groups
    me = lax.axis_index("space")
    towards = (lax.rem(me + count - 1, count), lax.rem(me + 1, count))

    if greet:
        barrier = pltpu.get_barrier_semaphore()
        for neighbour in towards:
            pl.semaphore_signal(barrier, inc=1, device_id={"space": neighbour}, device_id_type=MESH)

    def swap(step, group, side):
        number = 2 * (step * groups + group) + side
        if step == STEPS:
            source, target = last_send.at[group, side], last_recv.at[group, 1 - side]
        else:
            source, target = send.at[step, group, side], recv.at[step, group, 1 - side]
        return exchange("space", number, source, target, towards[side], send_sem, recv_sem)

    for group in range(groups):
        for side, row in ((UP, 0), (DOWN, rows - 1)):
            for i in range(each):
                for k in range(2):
                    at = slice(k * each + i, k * each + i + 1)
                    send[0, group, side, at, :] = fields[group * each + i, 1 + k, row : row + 1, :]
    if greet:
        pl.semaphore_wait(barrier, 2)
    for group in range(groups):
        for side in (UP, DOWN):
            swap(0, group, side).start()

    keep = 1.0 / (1.0 + DT * drag[...])
    flux_c[...] = 0.5 * DT * depth[...]
    keep_c[...] = keep
    turn_c[...] = DT * coriolis[...] * keep
    push_c[...] = 0.5 * DT * keep
    for side in (UP, DOWN):
        rim_depth, rim_coriolis, rim_drag = (rim[side, k : k + 1, :] for k in range(3))
        k = 1.0 / (1.0 + DT * rim_drag)
        for i in range(each):
            at = slice(side * each + i, side * each + i + 1)
            rim_c[0, at, :] = 0.5 * DT * rim_depth
            rim_c[1, at, :] = k
            rim_c[2, at, :] = DT * rim_coriolis * k
            rim_c[3, at, :] = 0.5 * DT * k
            rim_c[4, at, :] = 0.5 * DT * k if side == UP else -0.5 * DT * k

    chunk = min(512, width)
    chunks = [(start, pl.ds(start, chunk)) for start in range(0, width, chunk)]

    def arrived(step, group):
        for side in (UP, DOWN):
            swap(step, group, side).wait_recv()
        return last_recv.at[group] if step == STEPS else recv.at[step, group]

    def beside(step, group, come):
        for side in (UP, DOWN):
            at = slice(side * each, (side + 1) * each)
            near[at, :] = come[side, 0:each, :]
            far[at, :] = send[step, group, side, 0:each, :] - come[side, each : 2 * each, :]
        u, v = halo[group, 0], halo[group, 1]
        slope = column_difference(lambda low, high: near[:, low:high], 0, width, width, True)
        halo[group, 0] = u * rim_c[1] + v * rim_c[2] - rim_c[3] * slope
        halo[group, 1] = v * rim_c[1] - u * rim_c[2] - rim_c[4] * far[...]

    def along(p, i, come, at):
        return out[p, 2, :, at] - push_c[:, at] * row_difference(
            out[p, 0, :, at], come[UP, i : i + 1, at], come[DOWN, i : i + 1, at]
        )

    for step in range(1, STEPS + 1):
        old = fields if step == 1 else out
        for group in range(groups):
            come = arrived(step - 1, group)
            if step == 1:
                for side in (UP, DOWN):
                    for k in range(2):
                        halo[group, k, side * each : (side + 1) * each, :] = come[
                            side, k * each : (k + 1) * each, :
                        ]
            else:
                beside(step - 1, group, come)
            near[...] = rim_c[0] * halo[group, 1]
            for i in range(each):
                p = group * each + i
                for start, at in chunks:
                    if step == 1:
                        v = fields[p, 2, :, at]
                    else:
                        v = along(p, i, come, at)
                        out[p, 2, :, at] = v
                    outflow = column_difference(
                        lambda low, high: flux_c[:, low:high] * old[p, 1, :, low:high], start, chunk, width, False
                    )
                    height = old[p, 0, :, at] - (
                        outflow
                        + row_difference(flux_c[:, at] * v, near[i : i + 1, at], near[each + i : each + i + 1, at])
                    )
                    out[p, 0, :, at] = height
                    if step == STEPS:
                        last_send[group, UP, i : i + 1, at] = height[0:1, :]
                        last_send[group, DOWN, i : i + 1, at] = height[rows - 1 : rows, :]
                    else:
                        for k in range(2):
                            n = k * each + i
                            send[step, group, UP, n : n + 1, at] = height[k : k + 1, :]
                            send[step, group, DOWN, n : n + 1, at] = height[rows - 1 - k : rows - k, :]
            for side in (UP, DOWN):
                swap(step, group, side).start()
            for i in range(each):
                p = group * each + i
                for start, at in chunks:
                    u, v = old[p, 1, :, at], (old if step == 1 else out)[p, 2, :, at]
                    slope = column_difference(
                        lambda low, high: out[p, 0, :, low:high], start, chunk, width, True
                    )
                    out[p, 1, :, at] = u * keep_c[:, at] + turn_c[:, at] * v - push_c[:, at] * slope
                    out[p, 2, :, at] = v * keep_c[:, at] - turn_c[:, at] * u
    for group in range(groups):
        come = arrived(STEPS, group)
        for i in range(each):
            p = group * each + i
            for start, at in chunks:
                out[p, 2, :, at] = along(p, i, come, at)
    for step in range(STEPS + 1):
        for group in range(groups):
            for side in (UP, DOWN):
                swap(step, group, side).wait_send()


def advance_scratch(members, rows, width, groups):
    each = members // groups
    f32 = jnp.float32
    plane = pltpu.VMEM((rows, width), f32)
    edges = pltpu.VMEM((2 * each, width), f32)
    copies = 2 * (STEPS + 1) * groups
    return [
        plane, plane, plane, plane,
        pltpu.VMEM((5, 2 * each, width), f32),
        pltpu.VMEM((STEPS, groups, 2, 2 * each, width), f32),
        pltpu.VMEM((STEPS, groups, 2, 2 * each, width), f32),
        pltpu.VMEM((groups, 2, each, width), f32),
        pltpu.VMEM((groups, 2, each, width), f32),
        pltpu.VMEM((groups, 2, 2 * each, width), f32),
        edges, edges,
        pltpu.SemaphoreType.DMA((copies,)),
        pltpu.SemaphoreType.DMA((copies,)),
    ]


def advance(fields, depth, coriolis, drag, rim, count):
    members, _, rows, width = fields.shape
    groups = members
    return pl.pallas_call(
        functools.partial(advance_kernel, count, groups, True),
        out_shape=jax.ShapeDtypeStruct(fields.shape, jnp.float32),
        in_specs=[pl.BlockSpec(memory_space=pltpu.VMEM)] * 5,
        out_specs=pl.BlockSpec(memory_space=pltpu.VMEM),
        scratch_shapes=advance_scratch(members, rows, width, groups),
        compiler_params=pltpu.CompilerParams(
            collective_id=0, has_side_effects=True, vmem_limit_bytes=40 * 1024 * 1024
        ),
        name="advance",
    )(fields, depth, coriolis, drag, rim)


def routes_kernel(members, across, out, tier_out):
    part = across.shape[1]
    me = lax.axis_index("dom")
    chip = me // 2
    lane = lax.broadcasted_iota(jnp.int32, (part, part), 1)
    sub = lax.broadcasted_iota(jnp.int32, (part, part), 0)
    row_p, col_p = lane[0:1, :], sub[:, 0:1]
    down = jnp.sum(jnp.where(lane == sub, across[...], 0), axis=1, keepdims=True)

    def over(mask, value, axis):
        return jnp.sum(jnp.where(mask, value, 0), axis=axis, keepdims=True)

    target_row = over((down == lane) & (sub != lane), sub + 1, 0) - 1
    target_col = over((across[...] == sub) & (sub != lane), lane + 1, 1) - 1

    def chip_of(p):
        return lax.shift_right_arithmetic(p, (2 * members).bit_length() - 1)

    def block_of(p):
        return lax.shift_right_arithmetic(p, members.bit_length() - 1)

    d_row = jnp.where(target_row >= 0, chip_of(row_p) ^ chip_of(target_row), 0)
    d_col = jnp.where(target_col >= 0, chip_of(col_p) ^ chip_of(target_col), 0)
    rank = over((target_col >= 0) & (sub < lane) & (block_of(sub) == block_of(lane)), 1, 0)
    own = (block_of(row_p) & 1) * CAP + rank

    columns = [None] * 8
    most_first, most_second = jnp.int32(0), jnp.int32(0)
    for q in range(2):
        first, second = 1 + q, 2 - q
        f_row, f_col = (d_row & first) != 0, (d_col & first) != 0
        g_row, g_col = (d_row & second) != 0, (d_col & second) != 0
        s1 = over(f_col & (chip_of(sub) == chip_of(lane)) & (sub < lane), 1, 0)
        e_row = chip_of(row_p) ^ (d_row & first)
        e_col = chip_of(col_p) ^ (d_col & first)
        key_row = row_p + jnp.where(f_row, part, 0)
        key_col = col_p + jnp.where(f_col, part, 0)
        s2 = over(g_col & (e_col == e_row) & (key_col < key_row), 1, 0)
        found = jnp.where(g_row, 4 * CAP + s2, jnp.where(f_row, 2 * CAP + s1, own))
        columns[q] = over((s1 == sub) & f_row & (chip_of(row_p) == chip), own, 1)
        columns[2 + q] = over(
            (s2 == sub) & g_row & (e_row == chip), jnp.where(f_row, 2 * CAP + s1, own), 1
        )
        columns[4 + q] = over(target_row == sub, found, 1)
        most_first = jnp.maximum(most_first, jnp.max(jnp.where(f_row, s1 + 1, 0)))
        most_second = jnp.maximum(most_second, jnp.max(jnp.where(g_row, s2 + 1, 0)))
    columns[6] = jnp.where(down != col_p, 1, 0)
    tier = jnp.int32(len(TIERS))
    for n in range(len(TIERS) - 1, -1, -1):
        fits = (most_first <= TIERS[n][0]) & (most_second <= TIERS[n][1])
        tier = jnp.where(fits, n, tier)
    mine = over((rank == sub) & (target_row >= 0) & (block_of(row_p) == me), row_p & (members - 1), 1)
    columns[7] = mine
    tier_out[0] = tier
    for k in range(8):
        out[:, k : k + 1] = columns[k]


TIERS = ((3, 3), (4, 4))
PIECES = 4


def resample_kernel(
    c1, c2, count,
    table, state, jitter, depth, coriolis, drag, out, rim,
    rim_send, core_send, last_send, last_recv, own_all, first_send_all, first_recv_all, second_send_all, second_recv_all,
    send_sem, recv_sem, rim_send_sem, rim_recv_sem,
):
    members, _, rows, width = out.shape
    half, wide = rows // 2, width // PIECES
    pieces = range(PIECES)
    me = lax.axis_index("dom")
    core = lax.rem(me, 2)
    chip = me // 2
    other = me + 1 - 2 * core
    turned = (me + 2 - 4 * lax.rem(chip, 2), me + 4 - 8 * (chip // 2))
    slab = lax.axis_index("space")
    towards = (lax.rem(slab + count - 1, count), lax.rem(slab + 1, count))
    mine, theirs = pl.multiple_of(core * half, half), pl.multiple_of((1 - core) * half, half)

    barrier = pltpu.get_barrier_semaphore()
    for device in (other,) + turned:
        pl.semaphore_signal(barrier, inc=1, device_id={"dom": device}, device_id_type=MESH)
    for neighbour in towards:
        pl.semaphore_signal(barrier, inc=1, device_id={"space": neighbour}, device_id_type=MESH)

    def send(number, source, target, device):
        return exchange("dom", number, source, target, device, send_sem, recv_sem)

    rims = [
        exchange("space", side, rim_send.at[side], rim.at[1 - side], towards[side], rim_send_sem, rim_recv_sem)
        for side in (UP, DOWN)
    ]
    own, first_send, first_recv, second_send, second_recv = (
        tuple(ref for ref in refs) for refs in
        (own_all, first_send_all, first_recv_all, second_send_all, second_recv_all)
    )
    cores = [send(t, core_send.at[t], own[t].at[pl.ds(core * CAP, CAP)], other) for t in pieces]
    firsts = [send(PIECES + t, first_send[t], first_recv[t], turned[t % 2]) for t in pieces]
    seconds = [send(2 * PIECES + t, second_send[t], second_recv[t], turned[1 - t % 2]) for t in pieces]
    lasts = [send(3 * PIECES + t, last_send.at[t], last_recv.at[t], other) for t in pieces]

    for side, row in ((UP, 0), (DOWN, rows - 1)):
        for k, plane in enumerate((depth, coriolis, drag, drag)):
            rim_send[side, k : k + 1, :] = plane[row : row + 1, :]
    for t in pieces:
        columns = pl.ds(t * wide, wide)
        for k in range(CAP):
            slot = table[k, 7]
            core_send[t, k] = state[slot, :, pl.ds(theirs, half), columns]
            own[t][core * CAP + k] = state[slot, :, pl.ds(mine, half), columns]
    pl.semaphore_wait(barrier, 5)
    for t in pieces:
        cores[t].start()
    for copy in rims:
        copy.start()
    for t in pieces:
        cores[t].wait_recv()
        for k in range(c1):
            first_send[t][k] = own[t][table[k, t % 2]]
        firsts[t].start()

    def pick(t, index, come):
        value = own[t][jnp.clip(index, 0, 2 * CAP - 1)]
        value = jnp.where(index >= 2 * CAP, first_recv[t][jnp.clip(index - 2 * CAP, 0, c1 - 1)], value)
        if come:
            value = jnp.where(
                index >= 4 * CAP, second_recv[t][jnp.clip(index - 4 * CAP, 0, c2 - 1)], value
            )
        return value

    for t in pieces:
        firsts[t].wait_recv()
        for k in range(c2):
            second_send[t][k] = pick(t, table[k, 2 + t % 2], False)
        seconds[t].start()
    for t in pieces:
        seconds[t].wait_recv()
        for k in range(members):
            last_send[t, k] = pick(t, table[other * members + k, 4 + t % 2], True)
        lasts[t].start()
        columns = pl.ds(t * wide, wide)
        for k in range(members):
            got = pick(t, table[me * members + k, 4 + t % 2], True)
            kept = state[k, :, pl.ds(mine, half), columns]
            out[k, :, pl.ds(mine, half), columns] = (
                jnp.where(table[me * members + k, 6] != 0, got, kept) + jitter[k, :, pl.ds(mine, half), columns]
            )
    for t in pieces:
        lasts[t].wait_recv()
        columns = pl.ds(t * wide, wide)
        for k in range(members):
            kept = state[k, :, pl.ds(theirs, half), columns]
            out[k, :, pl.ds(theirs, half), columns] = (
                jnp.where(table[me * members + k, 6] != 0, last_recv[t, k], kept)
                + jitter[k, :, pl.ds(theirs, half), columns]
            )
    for copy in rims:
        copy.wait()
    for copy in cores + firsts + seconds + lasts:
        copy.wait_send()


def cycle_kernel(c1, c2, count, groups, table, state, jitter, depth, coriolis, drag, out, rim, *scratch):
    first = len(scratch) - len(advance_scratch(4, 16, 2048, groups))
    resample_kernel(c1, c2, count, table, state, jitter, depth, coriolis, drag, out, rim, *scratch[:first])
    advance_kernel(count, groups, False, out, depth, coriolis, drag, rim, out, *scratch[first:])


def cycle(number, c1, c2, count, table, state, jitter, depth, coriolis, drag):
    members, parts, rows, width = state.shape
    groups = members
    f32 = jnp.float32
    vmem = pl.BlockSpec(memory_space=pltpu.VMEM)

    def slots(*lead):
        return pltpu.VMEM((*lead, parts, rows // 2, width // PIECES), f32)

    return pl.pallas_call(
        functools.partial(cycle_kernel, c1, c2, count, groups),
        out_shape=jax.ShapeDtypeStruct(state.shape, f32),
        in_specs=[pl.BlockSpec(memory_space=pltpu.SMEM)] + [vmem] * 5,
        out_specs=vmem,
        scratch_shapes=[
            pltpu.VMEM((2, 4, width), f32),
            pltpu.VMEM((2, 4, width), f32),
            slots(PIECES, CAP), slots(PIECES, members), slots(PIECES, members),
            [slots(2 * CAP)] * PIECES, [slots(c1)] * PIECES, [slots(c1)] * PIECES,
            [slots(c2)] * PIECES, [slots(c2)] * PIECES,
            pltpu.SemaphoreType.DMA((4 * PIECES,)), pltpu.SemaphoreType.DMA((4 * PIECES,)),
            pltpu.SemaphoreType.DMA((2,)), pltpu.SemaphoreType.DMA((2,)),
        ]
        + advance_scratch(members, rows, width, groups),
        compiler_params=pltpu.CompilerParams(
            collective_id=number, has_side_effects=True, vmem_limit_bytes=40 * 1024 * 1024
        ),
        name="cycle",
    )(table, state, jitter, depth, coriolis, drag)


def routed(count, ancestor, state, jitter, *planes):
    members = state.shape[0]
    part = ancestor.shape[0]
    table, tier = pl.pallas_call(
        functools.partial(routes_kernel, members),
        out_shape=(
            jax.ShapeDtypeStruct((part, 8), jnp.int32), jax.ShapeDtypeStruct((1,), jnp.int32),
        ),
        in_specs=[pl.BlockSpec(memory_space=pltpu.VMEM)],
        out_specs=(pl.BlockSpec(memory_space=pltpu.VMEM), pl.BlockSpec(memory_space=pltpu.SMEM)),
        name="routes",
    )(ancestor[None, :])
    sizes = TIERS + ((2 * CAP, 2 * members),)
    return lax.switch(
        tier[0],
        [functools.partial(cycle, 1 + n, c1, c2, count) for n, (c1, c2) in enumerate(sizes)],
        table, state, jitter, *planes,
    )


def edge_rows(count, *planes):
    stacked = jnp.stack(planes + planes[-1:])
    after = [(i, (i + 1) % count) for i in range(count)]
    before = [((i + 1) % count, i) for i in range(count)]
    return jnp.stack(
        [lax.ppermute(stacked[:, -1], "space", after), lax.ppermute(stacked[:, 0], "space", before)]
    )


def gathered(ancestor, state, jitter):
    members = state.shape[0]
    part = ancestor.shape[0]
    first = lax.axis_index("dom") * members
    index = jnp.arange(part, dtype=jnp.int32)
    moved = ancestor != index
    donor = jnp.any((ancestor[:, None] == index[None, :]) & moved[:, None], axis=0)
    earlier = (index[None, :] < index[:, None]) & (index[None, :] // members == index[:, None] // members)
    place = jnp.sum((earlier & donor[None, :]).astype(jnp.int32), axis=1)
    sent = []
    for k in range(CAP):
        hit = donor & (place == k) & (index // members == first // members)
        slot = jnp.sum(jnp.where(hit, index - first, 0))
        sent.append(lax.dynamic_slice_in_dim(state, slot, 1))
    pool = lax.all_gather(jnp.concatenate(sent), "dom", axis=0, tiled=True)
    where = (ancestor // members) * CAP + jnp.sum(
        jnp.where(ancestor[:, None] == index[None, :], place[None, :], 0), axis=1
    )
    copied = []
    for k in range(members):
        j = first + k
        got = lax.dynamic_slice_in_dim(pool, where[j], 1)
        copied.append(jnp.where(moved[j], got, state[k : k + 1]))
    return jnp.concatenate(copied) + jitter


def local(count, doms, ancestor, state, jitter, depth, coriolis, drag):
    members = state.shape[0]
    simple = doms == 8 and members == 4 and state.shape[2] % 16 == 0
    planes = (depth, coriolis, drag)
    if simple:
        return routed(count, ancestor, state, jitter, *planes)
    return advance(gathered(ancestor, state, jitter), *planes, edge_rows(count, *planes), count)


def solution(mesh):
    field = P("dom", None, "space", None)
    plane = P("space", None)
    return jax.shard_map(
        functools.partial(local, mesh.shape["space"], mesh.shape["dom"]),
        mesh=mesh,
        in_specs=(P(), field, field, plane, plane, plane),
        out_specs=field,
        check_vma=False,
    )
```

```python
import functools

import jax
import jax.numpy as jnp
from jax import lax
from jax.experimental import pallas as pl
from jax.experimental.pallas import tpu as pltpu
from jax.sharding import PartitionSpec as P

STEPS = 4
DT = 0.3
CAP = 2
MESH = pl.DeviceIdType.MESH
UP, DOWN = 0, 1


def column_difference(load, start, size, width, edge):
    low, high = max(start - 128, 0), min(start + size + 128, width)
    a = load(low, high)
    after = pltpu.roll(a, high - low - 1, 1)[:, start - low : start - low + size]
    before = pltpu.roll(a, 1, 1)[:, start - low : start - low + size]
    if low == start or high == start + size:
        here = a[:, start - low : start - low + size]
        beyond = here if edge else jnp.zeros_like(here)
        column = lax.broadcasted_iota(jnp.int32, here.shape, 1)
        if high == start + size:
            after = jnp.where(column == size - 1, beyond, after)
        if low == start:
            before = jnp.where(column == 0, beyond, before)
    return after - before


def row_difference(a, above, below):
    rows = a.shape[0]
    row = lax.broadcasted_iota(jnp.int32, a.shape, 0)
    after = jnp.where(row == rows - 1, below, pltpu.roll(a, rows - 1, 0))
    before = jnp.where(row == 0, above, pltpu.roll(a, 1, 0))
    return after - before


def exchange(axis, number, source, target, device, send_sem, recv_sem):
    return pltpu.make_async_remote_copy(
        src_ref=source, dst_ref=target, send_sem=send_sem.at[number], recv_sem=recv_sem.at[number],
        device_id={axis: device}, device_id_type=MESH,
    )


def advance_kernel(
    count, groups, greet,
    fields, depth, coriolis, drag, rim, out,
    flux_c, keep_c, turn_c, push_c, rim_c, send, recv, last_send, last_recv, halo, near, far,
    send_sem, recv_sem,
):
    members, _, rows, width = out.shape
    each = members // groups
    me = lax.axis_index("space")
    towards = (lax.rem(me + count - 1, count), lax.rem(me + 1, count))

    if greet:
        barrier = pltpu.get_barrier_semaphore()
        for neighbour in towards:
            pl.semaphore_signal(barrier, inc=1, device_id={"space": neighbour}, device_id_type=MESH)

    def swap(step, group, side):
        number = 2 * (step * groups + group) + side
        if step == STEPS:
            source, target = last_send.at[group, side], last_recv.at[group, 1 - side]
        else:
            source, target = send.at[step, group, side], recv.at[step, group, 1 - side]
        return exchange("space", number, source, target, towards[side], send_sem, recv_sem)

    for group in range(groups):
        for side, row in ((UP, 0), (DOWN, rows - 1)):
            for i in range(each):
                for k in range(2):
                    at = slice(k * each + i, k * each + i + 1)
                    send[0, group, side, at, :] = fields[group * each + i, 1 + k, row : row + 1, :]
    if greet:
        pl.semaphore_wait(barrier, 2)
    for group in range(groups):
        for side in (UP, DOWN):
            swap(0, group, side).start()

    keep = 1.0 / (1.0 + DT * drag[...])
    flux_c[...] = 0.5 * DT * depth[...]
    keep_c[...] = keep
    turn_c[...] = DT * coriolis[...] * keep
    push_c[...] = 0.5 * DT * keep
    for side in (UP, DOWN):
        rim_depth, rim_coriolis, rim_drag = (rim[side, k : k + 1, :] for k in range(3))
        k = 1.0 / (1.0 + DT * rim_drag)
        for i in range(each):
            at = slice(side * each + i, side * each + i + 1)
            rim_c[0, at, :] = 0.5 * DT * rim_depth
            rim_c[1, at, :] = k
            rim_c[2, at, :] = DT * rim_coriolis * k
            rim_c[3, at, :] = 0.5 * DT * k
            rim_c[4, at, :] = 0.5 * DT * k if side == UP else -0.5 * DT * k

    chunk = min(512, width)
    chunks = [(start, pl.ds(start, chunk)) for start in range(0, width, chunk)]

    def arrived(step, group):
        for side in (UP, DOWN):
            swap(step, group, side).wait_recv()
        return last_recv.at[group] if step == STEPS else recv.at[step, group]

    def beside(step, group, come):
        for side in (UP, DOWN):
            at = slice(side * each, (side + 1) * each)
            near[at, :] = come[side, 0:each, :]
            far[at, :] = send[step, group, side, 0:each, :] - come[side, each : 2 * each, :]
        u, v = halo[group, 0], halo[group, 1]
        slope = column_difference(lambda low, high: near[:, low:high], 0, width, width, True)
        halo[group, 0] = u * rim_c[1] + v * rim_c[2] - rim_c[3] * slope
        halo[group, 1] = v * rim_c[1] - u * rim_c[2] - rim_c[4] * far[...]

    def along(p, i, come, at):
        return out[p, 2, :, at] - push_c[:, at] * row_difference(
            out[p, 0, :, at], come[UP, i : i + 1, at], come[DOWN, i : i + 1, at]
        )

    for step in range(1, STEPS + 1):
        old = fields if step == 1 else out
        def forward(group, carry, step=step, old=old):
            come = arrived(step - 1, group)
            if step == 1:
                for side in (UP, DOWN):
                    for k in range(2):
                        halo[group, k, side * each : (side + 1) * each, :] = come[
                            side, k * each : (k + 1) * each, :
                        ]
            else:
                beside(step - 1, group, come)
            near[...] = rim_c[0] * halo[group, 1]
            for i in range(each):
                p = group * each + i
                for start, at in chunks:
                    if step == 1:
                        v = fields[p, 2, :, at]
                    else:
                        v = along(p, i, come, at)
                        out[p, 2, :, at] = v
                    outflow = column_difference(
                        lambda low, high: flux_c[:, low:high] * old[p, 1, :, low:high], start, chunk, width, False
                    )
                    height = old[p, 0, :, at] - (
                        outflow
                        + row_difference(flux_c[:, at] * v, near[i : i + 1, at], near[each + i : each + i + 1, at])
                    )
                    out[p, 0, :, at] = height
                    if step == STEPS:
                        last_send[group, UP, i : i + 1, at] = height[0:1, :]
                        last_send[group, DOWN, i : i + 1, at] = height[rows - 1 : rows, :]
                    else:
                        for k in range(2):
                            n = k * each + i
                            send[step, group, UP, n : n + 1, at] = height[k : k + 1, :]
                            send[step, group, DOWN, n : n + 1, at] = height[rows - 1 - k : rows - k, :]
            for side in (UP, DOWN):
                swap(step, group, side).start()
            for i in range(each):
                p = group * each + i
                for start, at in chunks:
                    u, v = old[p, 1, :, at], (old if step == 1 else out)[p, 2, :, at]
                    slope = column_difference(
                        lambda low, high: out[p, 0, :, low:high], start, chunk, width, True
                    )
                    out[p, 1, :, at] = u * keep_c[:, at] + turn_c[:, at] * v - push_c[:, at] * slope
                    out[p, 2, :, at] = v * keep_c[:, at] - turn_c[:, at] * u
            return carry

        lax.fori_loop(0, groups, forward, 0)

    def close(group, carry):
        come = arrived(STEPS, group)
        for i in range(each):
            p = group * each + i
            for start, at in chunks:
                out[p, 2, :, at] = along(p, i, come, at)
        return carry

    lax.fori_loop(0, groups, close, 0)
    for step in range(STEPS + 1):
        for group in range(groups):
            for side in (UP, DOWN):
                swap(step, group, side).wait_send()


def advance_scratch(members, rows, width, groups):
    each = members // groups
    f32 = jnp.float32
    plane = pltpu.VMEM((rows, width), f32)
    edges = pltpu.VMEM((2 * each, width), f32)
    copies = 2 * (STEPS + 1) * groups
    return [
        plane, plane, plane, plane,
        pltpu.VMEM((5, 2 * each, width), f32),
        pltpu.VMEM((STEPS, groups, 2, 2 * each, width), f32),
        pltpu.VMEM((STEPS, groups, 2, 2 * each, width), f32),
        pltpu.VMEM((groups, 2, each, width), f32),
        pltpu.VMEM((groups, 2, each, width), f32),
        pltpu.VMEM((groups, 2, 2 * each, width), f32),
        edges, edges,
        pltpu.SemaphoreType.DMA((copies,)),
        pltpu.SemaphoreType.DMA((copies,)),
    ]


def advance(fields, depth, coriolis, drag, rim, count):
    members, _, rows, width = fields.shape
    groups = members
    return pl.pallas_call(
        functools.partial(advance_kernel, count, groups, True),
        out_shape=jax.ShapeDtypeStruct(fields.shape, jnp.float32),
        in_specs=[pl.BlockSpec(memory_space=pltpu.VMEM)] * 5,
        out_specs=pl.BlockSpec(memory_space=pltpu.VMEM),
        scratch_shapes=advance_scratch(members, rows, width, groups),
        compiler_params=pltpu.CompilerParams(
            collective_id=0, has_side_effects=True, vmem_limit_bytes=40 * 1024 * 1024
        ),
        name="advance",
    )(fields, depth, coriolis, drag, rim)


def routes_kernel(members, across, out, tier_out):
    part = across.shape[1]
    me = lax.axis_index("dom")
    chip = me // 2
    lane = lax.broadcasted_iota(jnp.int32, (part, part), 1)
    sub = lax.broadcasted_iota(jnp.int32, (part, part), 0)
    row_p, col_p = lane[0:1, :], sub[:, 0:1]
    down = jnp.sum(jnp.where(lane == sub, across[...], 0), axis=1, keepdims=True)

    def over(mask, value, axis):
        return jnp.sum(jnp.where(mask, value, 0), axis=axis, keepdims=True)

    target_row = over((down == lane) & (sub != lane), sub + 1, 0) - 1
    target_col = over((across[...] == sub) & (sub != lane), lane + 1, 1) - 1

    def chip_of(p):
        return lax.shift_right_arithmetic(p, (2 * members).bit_length() - 1)

    def block_of(p):
        return lax.shift_right_arithmetic(p, members.bit_length() - 1)

    d_row = jnp.where(target_row >= 0, chip_of(row_p) ^ chip_of(target_row), 0)
    d_col = jnp.where(target_col >= 0, chip_of(col_p) ^ chip_of(target_col), 0)
    rank = over((target_col >= 0) & (sub < lane) & (block_of(sub) == block_of(lane)), 1, 0)
    own = (block_of(row_p) & 1) * CAP + rank

    columns = [None] * 8
    most_first, most_second = jnp.int32(0), jnp.int32(0)
    for q in range(2):
        first, second = 1 + q, 2 - q
        f_row, f_col = (d_row & first) != 0, (d_col & first) != 0
        g_row, g_col = (d_row & second) != 0, (d_col & second) != 0
        s1 = over(f_col & (chip_of(sub) == chip_of(lane)) & (sub < lane), 1, 0)
        e_row = chip_of(row_p) ^ (d_row & first)
        e_col = chip_of(col_p) ^ (d_col & first)
        key_row = row_p + jnp.where(f_row, part, 0)
        key_col = col_p + jnp.where(f_col, part, 0)
        s2 = over(g_col & (e_col == e_row) & (key_col < key_row), 1, 0)
        found = jnp.where(g_row, 4 * CAP + s2, jnp.where(f_row, 2 * CAP + s1, own))
        columns[q] = over((s1 == sub) & f_row & (chip_of(row_p) == chip), own, 1)
        columns[2 + q] = over(
            (s2 == sub) & g_row & (e_row == chip), jnp.where(f_row, 2 * CAP + s1, own), 1
        )
        columns[4 + q] = over(target_row == sub, found, 1)
        most_first = jnp.maximum(most_first, jnp.max(jnp.where(f_row, s1 + 1, 0)))
        most_second = jnp.maximum(most_second, jnp.max(jnp.where(g_row, s2 + 1, 0)))
    columns[6] = jnp.where(down != col_p, 1, 0)
    tier = jnp.int32(len(TIERS))
    for n in range(len(TIERS) - 1, -1, -1):
        fits = (most_first <= TIERS[n][0]) & (most_second <= TIERS[n][1])
        tier = jnp.where(fits, n, tier)
    mine = over((rank == sub) & (target_row >= 0) & (block_of(row_p) == me), row_p & (members - 1), 1)
    columns[7] = mine
    tier_out[0] = tier
    for k in range(8):
        out[:, k : k + 1] = columns[k]


TIERS = ((3, 3), (4, 4))
PIECES = 4


def resample_kernel(
    c1, c2, count,
    table, state, jitter, depth, coriolis, drag, out, rim,
    rim_send, core_send, last_send, last_recv, own_all, first_send_all, first_recv_all, second_send_all, second_recv_all,
    send_sem, recv_sem, rim_send_sem, rim_recv_sem,
):
    members, _, rows, width = out.shape
    half, wide = rows // 2, width // PIECES
    pieces = range(PIECES)
    me = lax.axis_index("dom")
    core = lax.rem(me, 2)
    chip = me // 2
    other = me + 1 - 2 * core
    turned = (me + 2 - 4 * lax.rem(chip, 2), me + 4 - 8 * (chip // 2))
    slab = lax.axis_index("space")
    towards = (lax.rem(slab + count - 1, count), lax.rem(slab + 1, count))
    mine, theirs = pl.multiple_of(core * half, half), pl.multiple_of((1 - core) * half, half)

    barrier = pltpu.get_barrier_semaphore()
    for device in (other,) + turned:
        pl.semaphore_signal(barrier, inc=1, device_id={"dom": device}, device_id_type=MESH)
    for neighbour in towards:
        pl.semaphore_signal(barrier, inc=1, device_id={"space": neighbour}, device_id_type=MESH)

    def send(number, source, target, device):
        return exchange("dom", number, source, target, device, send_sem, recv_sem)

    rims = [
        exchange("space", side, rim_send.at[side], rim.at[1 - side], towards[side], rim_send_sem, rim_recv_sem)
        for side in (UP, DOWN)
    ]
    own, first_send, first_recv, second_send, second_recv = (
        tuple(ref for ref in refs) for refs in
        (own_all, first_send_all, first_recv_all, second_send_all, second_recv_all)
    )
    cores = [send(t, core_send.at[t], own[t].at[pl.ds(core * CAP, CAP)], other) for t in pieces]
    firsts = [send(PIECES + t, first_send[t], first_recv[t], turned[t % 2]) for t in pieces]
    seconds = [send(2 * PIECES + t, second_send[t], second_recv[t], turned[1 - t % 2]) for t in pieces]
    lasts = [send(3 * PIECES + t, last_send.at[t], last_recv.at[t], other) for t in pieces]

    for side, row in ((UP, 0), (DOWN, rows - 1)):
        for k, plane in enumerate((depth, coriolis, drag, drag)):
            rim_send[side, k : k + 1, :] = plane[row : row + 1, :]
    for t in pieces:
        columns = pl.ds(t * wide, wide)
        for k in range(CAP):
            slot = table[k, 7]
            core_send[t, k] = state[slot, :, pl.ds(theirs, half), columns]
            own[t][core * CAP + k] = state[slot, :, pl.ds(mine, half), columns]
    pl.semaphore_wait(barrier, 5)
    for t in pieces:
        cores[t].start()
    for copy in rims:
        copy.start()
    for t in pieces:
        cores[t].wait_recv()
        for k in range(c1):
            first_send[t][k] = own[t][table[k, t % 2]]
        firsts[t].start()

    def pick(t, index, come):
        value = own[t][jnp.clip(index, 0, 2 * CAP - 1)]
        value = jnp.where(index >= 2 * CAP, first_recv[t][jnp.clip(index - 2 * CAP, 0, c1 - 1)], value)
        if come:
            value = jnp.where(
                index >= 4 * CAP, second_recv[t][jnp.clip(index - 4 * CAP, 0, c2 - 1)], value
            )
        return value

    for t in pieces:
        firsts[t].wait_recv()
        for k in range(c2):
            second_send[t][k] = pick(t, table[k, 2 + t % 2], False)
        seconds[t].start()
    for t in pieces:
        seconds[t].wait_recv()
        for k in range(members):
            last_send[t, k] = pick(t, table[other * members + k, 4 + t % 2], True)
        lasts[t].start()
        columns = pl.ds(t * wide, wide)
        for k in range(members):
            got = pick(t, table[me * members + k, 4 + t % 2], True)
            kept = state[k, :, pl.ds(mine, half), columns]
            out[k, :, pl.ds(mine, half), columns] = (
                jnp.where(table[me * members + k, 6] != 0, got, kept) + jitter[k, :, pl.ds(mine, half), columns]
            )
    for t in pieces:
        lasts[t].wait_recv()
        columns = pl.ds(t * wide, wide)
        for k in range(members):
            kept = state[k, :, pl.ds(theirs, half), columns]
            out[k, :, pl.ds(theirs, half), columns] = (
                jnp.where(table[me * members + k, 6] != 0, last_recv[t, k], kept)
                + jitter[k, :, pl.ds(theirs, half), columns]
            )
    for copy in rims:
        copy.wait()
    for copy in cores + firsts + seconds + lasts:
        copy.wait_send()


def cycle_kernel(c1, c2, count, groups, table, state, jitter, depth, coriolis, drag, out, rim, *scratch):
    first = len(scratch) - len(advance_scratch(4, 16, 2048, groups))
    resample_kernel(c1, c2, count, table, state, jitter, depth, coriolis, drag, out, rim, *scratch[:first])
    advance_kernel(count, groups, False, out, depth, coriolis, drag, rim, out, *scratch[first:])


def cycle(number, c1, c2, count, table, state, jitter, depth, coriolis, drag):
    members, parts, rows, width = state.shape
    groups = members
    f32 = jnp.float32
    vmem = pl.BlockSpec(memory_space=pltpu.VMEM)

    def slots(*lead):
        return pltpu.VMEM((*lead, parts, rows // 2, width // PIECES), f32)

    return pl.pallas_call(
        functools.partial(cycle_kernel, c1, c2, count, groups),
        out_shape=jax.ShapeDtypeStruct(state.shape, f32),
        in_specs=[pl.BlockSpec(memory_space=pltpu.SMEM)] + [vmem] * 5,
        out_specs=vmem,
        scratch_shapes=[
            pltpu.VMEM((2, 4, width), f32),
            pltpu.VMEM((2, 4, width), f32),
            slots(PIECES, CAP), slots(PIECES, members), slots(PIECES, members),
            [slots(2 * CAP)] * PIECES, [slots(c1)] * PIECES, [slots(c1)] * PIECES,
            [slots(c2)] * PIECES, [slots(c2)] * PIECES,
            pltpu.SemaphoreType.DMA((4 * PIECES,)), pltpu.SemaphoreType.DMA((4 * PIECES,)),
            pltpu.SemaphoreType.DMA((2,)), pltpu.SemaphoreType.DMA((2,)),
        ]
        + advance_scratch(members, rows, width, groups),
        compiler_params=pltpu.CompilerParams(
            collective_id=number, has_side_effects=True, vmem_limit_bytes=40 * 1024 * 1024
        ),
        name="cycle",
    )(table, state, jitter, depth, coriolis, drag)


def routed(count, ancestor, state, jitter, *planes):
    members = state.shape[0]
    part = ancestor.shape[0]
    table, tier = pl.pallas_call(
        functools.partial(routes_kernel, members),
        out_shape=(
            jax.ShapeDtypeStruct((part, 8), jnp.int32), jax.ShapeDtypeStruct((1,), jnp.int32),
        ),
        in_specs=[pl.BlockSpec(memory_space=pltpu.VMEM)],
        out_specs=(pl.BlockSpec(memory_space=pltpu.VMEM), pl.BlockSpec(memory_space=pltpu.SMEM)),
        name="routes",
    )(ancestor[None, :])
    sizes = TIERS + ((2 * CAP, 2 * members),)
    return lax.switch(
        tier[0],
        [functools.partial(cycle, 1 + n, c1, c2, count) for n, (c1, c2) in enumerate(sizes)],
        table, state, jitter, *planes,
    )


def edge_rows(count, *planes):
    stacked = jnp.stack(planes + planes[-1:])
    after = [(i, (i + 1) % count) for i in range(count)]
    before = [((i + 1) % count, i) for i in range(count)]
    return jnp.stack(
        [lax.ppermute(stacked[:, -1], "space", after), lax.ppermute(stacked[:, 0], "space", before)]
    )


def gathered(ancestor, state, jitter):
    members = state.shape[0]
    part = ancestor.shape[0]
    first = lax.axis_index("dom") * members
    index = jnp.arange(part, dtype=jnp.int32)
    moved = ancestor != index
    donor = jnp.any((ancestor[:, None] == index[None, :]) & moved[:, None], axis=0)
    earlier = (index[None, :] < index[:, None]) & (index[None, :] // members == index[:, None] // members)
    place = jnp.sum((earlier & donor[None, :]).astype(jnp.int32), axis=1)
    sent = []
    for k in range(CAP):
        hit = donor & (place == k) & (index // members == first // members)
        slot = jnp.sum(jnp.where(hit, index - first, 0))
        sent.append(lax.dynamic_slice_in_dim(state, slot, 1))
    pool = lax.all_gather(jnp.concatenate(sent), "dom", axis=0, tiled=True)
    where = (ancestor // members) * CAP + jnp.sum(
        jnp.where(ancestor[:, None] == index[None, :], place[None, :], 0), axis=1
    )
    copied = []
    for k in range(members):
        j = first + k
        got = lax.dynamic_slice_in_dim(pool, where[j], 1)
        copied.append(jnp.where(moved[j], got, state[k : k + 1]))
    return jnp.concatenate(copied) + jitter


def local(count, doms, ancestor, state, jitter, depth, coriolis, drag):
    members = state.shape[0]
    simple = doms == 8 and members == 4 and state.shape[2] % 16 == 0
    planes = (depth, coriolis, drag)
    if simple:
        return routed(count, ancestor, state, jitter, *planes)
    return advance(gathered(ancestor, state, jitter), *planes, edge_rows(count, *planes), count)


def solution(mesh):
    field = P("dom", None, "space", None)
    plane = P("space", None)
    return jax.shard_map(
        functools.partial(local, mesh.shape["space"], mesh.shape["dom"]),
        mesh=mesh,
        in_specs=(P(), field, field, plane, plane, plane),
        out_specs=field,
        check_vma=False,
    )
```
